768 devices in a mesh: dp: 32 (over y, x), expert: 24 (over z, core).
Axes of the slice: x: 4, y: 8, z: 12, core: 2. Of those that a mesh axis runs over, the one named last changes fastest.
Arguments:
- tokens: bfloat16 [30720, 2048], P(('dp', 'expert')), may hold values from -6 to 6
- grad_out: bfloat16 [30720, 512], P(('dp', 'expert')), may hold values from -4 to 4
- routes: int32 [30720, 8], P(('dp', 'expert')), may hold values from 0 to 23, all different within a row; in each aligned block of 40 rows (0 to 39, 40 to 79, ...) at most 15 rows name the same one
- combine: bfloat16 [30720, 8], P(('dp', 'expert')), may hold values from 0.049804688 to 0.5
- w_gate: bfloat16 [24, 2048, 512], P('expert'), may hold values from -0.125 to 0.125
- w_up: bfloat16 [24, 2048, 512], P('expert'), may hold values from -0.125 to 0.125
Outputs:
- grad_tokens: bfloat16 [30720, 2048], P(('dp', 'expert'))
- grad_combine: bfloat16 [30720, 8], P(('dp', 'expert'))
- grad_gate: float32 [24, 2048, 512], P('expert', 'dp')
- grad_up: float32 [24, 2048, 512], P('expert', 'dp')
The draws below stay inside these ranges and needn't reach their ends.
Inputs may be any that keep to these rules, and one draw needn't show every extreme that they name: `routes`: among the rows of one device no expert is chosen more than 15 times; in every draw some expert is chosen exactly 15 times by one device's rows; the 8 experts of a token are different, and every expert is chosen somewhere.
All inputs are finite; a program needn't handle non-finite values.
Results may differ from the reference program's by a relative error of at most 0.02.
Values may be sent and summed in bfloat16 or wider, within the bound.
A program may use at most 64 MiB of HBM per device.

```python
import math
import jax
import jax.numpy as jnp
import numpy as np
from jax import lax

D = 2048
FF = 512
TOPK = 8
TOK_DEV = 40
EXPERTS = 24
CAP = 15
TOKENS = 30720
N_DP = 32
N_EXPERT = 24


def block_levels(key, dims, shards, least, high):
    def one(position, blocks):
        draws = jax.random.uniform(jax.random.fold_in(jax.random.fold_in(key, 6), position), (blocks,), jnp.float32, least / len(shards), high / len(shards))
        return jnp.repeat(jnp.exp(draws), dims[position] // blocks).reshape((-1,) + (1,) * (len(dims) - position - 1))

    loudness = one(*shards[0])
    for cut in shards[1:]:
        loudness = loudness * one(*cut)
    return loudness


def deal_out(own_key, own, number, rows, count, top, limit, skew):
    ranking = jax.random.permutation(own_key, count)
    packed, ordinary = portions_of(count, rows * top, limit, skew, True), portions_of(count, rows * top, limit, skew, False)
    places = jnp.arange(count)

    def named(tallies, turn):
        used = int((tallies > 0).sum())
        fixed = max(1, used // 4)
        moved = fixed + (places - fixed + turn * (used - fixed)) % max(1, count - fixed)
        return jnp.zeros((count,), jnp.int32).at[ranking[jnp.where(places < fixed, places, moved)]].set(jnp.asarray(tallies, jnp.int32))

    tallies = jnp.where(number % 4 == 0, named(packed, number // 4), named(ordinary, number - number // 4 - 1))
    mixed = jax.random.permutation(jax.random.fold_in(own, 3), count)
    source_of, taker = mixed[0:count // 2 * 2:2], mixed[1:count // 2 * 2:2]
    margin = jnp.minimum(tallies[source_of] - 1, limit - tallies[taker]) // 2
    margin = jnp.where((source_of == ranking[0]) | (taker == ranking[0]) | (tallies[taker] == 0), 0, jnp.maximum(margin, 0))
    moved = jax.random.randint(jax.random.fold_in(own, 4), (count // 2,), 0, 1 << 20) % (margin + 1)
    tallies = tallies.at[source_of].add(-moved).at[taker].add(moved)
    items = jnp.searchsorted(jnp.cumsum(tallies), jnp.arange(rows * top), side="right").astype(jnp.int32)
    listing = items.reshape(top, rows).T
    listing = listing[jax.random.permutation(jax.random.fold_in(own, 1), rows)]
    turn = jax.random.randint(jax.random.fold_in(own, 2), (rows, 1), 0, top)
    return jnp.take_along_axis(listing, (jnp.arange(top)[None, :] + turn) % top, axis=1)


def portions_of(amount, total, bound, skew, full):
    portions = [(1 << 20) // math.isqrt(rank ** skew) + 1 for rank in range(1, amount + 1)]
    largest = bound if full else min(bound, max(-(-total // amount), total * portions[0] // sum(portions)))
    least = 1 if total - largest >= amount - 1 else 0
    holding, spare = [largest] + [least] * (amount - 1), total - largest - least * (amount - 1)
    while spare > 0:
        movable = [i for i in range(1, amount) if holding[i] < largest] or [i for i in range(1, amount) if holding[i] < bound]
        pool, budget = sum([portions[i] for i in movable]), spare
        for i in movable:
            more = min(bound - holding[i], max(1, budget * portions[i] // pool), spare)
            holding[i] = holding[i] + more
            spare = spare - more
    return np.array(holding)


def centred(stream_key, extent, scale, reach, pieces=(), kind=jnp.bfloat16):
    values = jax.random.normal(stream_key, extent, jnp.float32) * scale
    if len(pieces) > 0:
        values = block_levels(stream_key, extent, pieces, -0.22, 0.18) * values
    return jnp.clip(values, min=-reach, max=reach).astype(kind)


def setup_inputs(seed: int = 0) -> dict:
    seeds = jax.random.split(jax.random.key(seed), 7)
    tokens = centred(seeds[0], (TOKENS, D), 1.0, 6.0, ((0, 768),))
    grad_out = centred(seeds[1], (TOKENS, FF), 0.5, 4.0, ((0, 768),))
    routes_keys = jax.random.split(jax.random.fold_in(seeds[2], 1), TOKENS // TOK_DEV)
    routes_turns = jax.random.permutation(jax.random.fold_in(seeds[2], 3), TOKENS // TOK_DEV)
    routes = jax.vmap(lambda own, number: deal_out(jax.random.fold_in(seeds[2], 2), own, number, TOK_DEV, EXPERTS, TOPK, CAP, 2))(routes_keys, routes_turns).reshape((TOKENS, TOPK))
    combine = jnp.clip(jnp.exp(math.log(0.5) - 2.306499 * jax.random.uniform(seeds[3], (TOKENS, TOPK), jnp.float32) ** block_levels(seeds[3], (TOKENS, TOPK), ((0, 768),), -0.2, 0.2)), 0.049804688, 0.5).astype(jnp.bfloat16)
    w_gate = centred(seeds[4], (EXPERTS, D, FF), D ** -0.5, 0.125, ((0, 24),))
    w_up = centred(seeds[5], (EXPERTS, D, FF), D ** -0.5, 0.125, ((0, 24),))
    return {"tokens": tokens, "grad_out": grad_out, "routes": routes, "combine": combine, "w_gate": w_gate, "w_up": w_up}


def reference(tokens, grad_out, routes, combine, w_gate, w_up):
    dev_count = N_DP * N_EXPERT
    per_device = TOK_DEV * TOPK
    chosen = routes.reshape(dev_count, per_device)
    one_hot = (chosen[:, :, None] == jnp.arange(EXPERTS, dtype=jnp.int32)[None, None, :]).astype(jnp.int32)
    rank_in = jnp.sum((jnp.cumsum(one_hot, axis=1) - one_hot) * one_hot, axis=2).astype(jnp.int32)
    slot_ids = (chosen * CAP + rank_in).astype(jnp.int32)
    device_ids = jnp.broadcast_to(jnp.arange(dev_count, dtype=jnp.int32)[:, None], (dev_count, per_device))
    entry_ids = jnp.broadcast_to(jnp.arange(per_device, dtype=jnp.int32)[None, :], (dev_count, per_device))
    slot_table = jnp.full((dev_count, EXPERTS * CAP), -1, dtype=jnp.int32)
    slot_table = slot_table.at[device_ids, slot_ids].set(entry_ids)
    slot_table = jnp.transpose(slot_table.reshape(dev_count, EXPERTS, CAP), (1, 0, 2))
    token_blocks = tokens.reshape(dev_count, TOK_DEV, D)
    grad_blocks = grad_out.reshape(dev_count, TOK_DEV, FF)
    weight_blocks = combine.reshape(dev_count, per_device)
    source = jnp.arange(dev_count, dtype=jnp.int32)[:, None]

    def expert_step(state_pair, inputs):
        token_sum, combine_sum = state_pair
        entries, gate_matrix, up_matrix = inputs
        is_valid = entries >= 0
        entry_safe = jnp.where(is_valid, entries, 0).astype(jnp.int32)
        row_ids = (entry_safe // TOPK).astype(jnp.int32)
        rows_in = token_blocks[source, row_ids].astype(jnp.float32)
        grads_in = grad_blocks[source, row_ids].astype(jnp.float32)
        weights_in = jnp.where(is_valid, weight_blocks[source, entry_safe].astype(jnp.float32), jnp.float32(0.0))
        gate_float = gate_matrix.astype(jnp.float32)
        up_float = up_matrix.astype(jnp.float32)
        gate_pre = jnp.einsum('ncd,df->ncf', rows_in, gate_float)
        up_pre = jnp.einsum('ncd,df->ncf', rows_in, up_float)
        sigmoid_gate = jax.nn.sigmoid(gate_pre)
        activated = gate_pre * sigmoid_gate
        hidden = activated * up_pre
        upstream = weights_in[:, :, None] * grads_in
        combine_grad = jnp.sum(hidden * grads_in, axis=2).astype(jnp.bfloat16)
        gate_grad = (upstream * up_pre * sigmoid_gate * (1.0 + gate_pre * (1.0 - sigmoid_gate))).astype(jnp.bfloat16)
        up_grad = (upstream * activated).astype(jnp.bfloat16)
        gate_back = gate_grad.astype(jnp.float32)
        up_back = up_grad.astype(jnp.float32)
        input_grad = (jnp.einsum('ncf,df->ncd', gate_back, gate_float) + jnp.einsum('ncf,df->ncd', up_back, up_float)).astype(jnp.bfloat16)
        flat_rows = jnp.where(is_valid, source * TOK_DEV + row_ids, dev_count * TOK_DEV).astype(jnp.int32)
        token_sum = token_sum.at[flat_rows].add(input_grad.astype(jnp.float32), mode='drop')
        flat_entries = jnp.where(is_valid, source * per_device + entry_safe, dev_count * per_device).astype(jnp.int32)
        combine_sum = combine_sum.at[flat_entries].add(combine_grad.astype(jnp.float32), mode='drop')
        row_view = rows_in.reshape(N_DP, N_EXPERT * CAP, D)
        gate_parts = jnp.einsum('prd,prf->pdf', row_view, gate_back.reshape(N_DP, N_EXPERT * CAP, FF))
        up_parts = jnp.einsum('prd,prf->pdf', row_view, up_back.reshape(N_DP, N_EXPERT * CAP, FF))
        gate_total = jnp.sum(lax.optimization_barrier(gate_parts.astype(jnp.bfloat16)).astype(jnp.float32), axis=0)
        up_total = jnp.sum(lax.optimization_barrier(up_parts.astype(jnp.bfloat16)).astype(jnp.float32), axis=0)
        return (token_sum, combine_sum), (gate_total, up_total)

    start_state = (jnp.zeros((dev_count * TOK_DEV, D), jnp.float32), jnp.zeros((dev_count * per_device,), jnp.float32))
    final_state, stacked = lax.scan(expert_step, start_state, (slot_table, w_gate, w_up))
    token_sum, combine_sum = final_state
    grad_tokens = token_sum.astype(jnp.bfloat16)
    grad_combine = combine_sum.reshape(TOKENS, TOPK).astype(jnp.bfloat16)
    return grad_tokens, grad_combine, stacked[0], stacked[1]
```

```python
import functools

import jax
import jax.numpy as jnp
from jax import lax
from jax.experimental import pallas as pl
from jax.experimental.pallas import tpu as pltpu
from jax.sharding import PartitionSpec as P

F32 = jnp.float32
BF16 = jnp.bfloat16
MESH = pl.DeviceIdType.MESH

NX, NY, NZ = 4, 8, 12
TOK = 40
DM = 2048
FF = 512
AG_ROWS = (416, 400)
RS_ROWS = (336, 320)
CA = 640
CB = 2 * FF - CA
NT = (((1,), (1,)), ((), ()))
TN = (((0,), (0,)), ((), ()))


def dot(a, b, dims=(((1,), (0,)), ((), ()))):
    return lax.dot_general(a, b, dims, preferred_element_type=F32)


def iota(shape, dim):
    return lax.broadcasted_iota(jnp.int32, shape, dim)


def kernel(
    tok, go, routes, comb, wg, wu,
    gt, gc, dg, du,
    ZR, ZS, X, GU, WC, OWN, SND, SIB, RP, RM,
    PA, PB, AX1, AX2, SA, SAB, AY1, AY, BY, SB, SBB, BX1, BX2, BXS,
    w_sem,
    ag_send, zr_recv, sf_send, zs_recv, snd_send, sib_recv, rs_send, rs_recv,
    ax1_send, ax1_recv, ax2_send, ax2_recv, ay_send, ay_recv, by_send, by_recv,
    bx1_send, bx1_recv, bx2_send, bx2_recv,
):
    dp = lax.axis_index("dp")
    ex = lax.axis_index("expert")
    x, y = lax.rem(dp, NX), dp // NX
    core, z = lax.rem(ex, 2), ex // 2

    def xdev(step):
        return (y * NX + lax.rem(x + step + NX, NX), ex)

    def ydev(step):
        return (lax.rem(y + step + NY, NY) * NX + x, ex)

    def zdev(step):
        return (dp, lax.rem(z + step + NZ, NZ) * 2 + core)

    sib = (dp, z * 2 + 1 - core)

    def remote(src, dst, ssem, rsem, dev):
        return pltpu.make_async_remote_copy(
            src_ref=src, dst_ref=dst, send_sem=ssem, recv_sem=rsem,
            device_id=dev, device_id_type=MESH,
        )

    load_g = pltpu.make_async_copy(wg.at[0], WC.at[:, pl.ds(0, FF)], w_sem.at[0])
    load_u = pltpu.make_async_copy(wu.at[0], WC.at[:, pl.ds(FF, FF)], w_sem.at[1])
    load_g.start()
    load_u.start()

    barrier = pltpu.get_barrier_semaphore()
    for dev in (zdev(1), zdev(-1), sib, xdev(1), xdev(-1), ydev(1), ydev(-1)):
        pl.semaphore_signal(barrier, inc=1, device_id=dev, device_id_type=MESH)

    tf = tok[...].astype(F32)
    gf = go[...].astype(F32)
    for j in range(2):
        for b in range(4):
            lo = j * 512 + b * 128
            ZR[0, j, pl.ds(80 * b, 80), :] = jnp.concatenate(
                [tf[:, lo:lo + 128], tf[:, 1024 + lo:1024 + lo + 128]], axis=0
            ).astype(BF16)
        ZR[0, j, pl.ds(320, 80), :] = jnp.concatenate(
            [gf[:, j * 128:j * 128 + 128], gf[:, 256 + j * 128:256 + j * 128 + 128]], axis=0
        ).astype(BF16)

    rt = routes[...]
    cf = comb[...].astype(F32)
    lane = iota((TOK, 128), 1)
    dense = jnp.zeros((TOK, 128), F32)
    for k in range(8):
        dense = dense + jnp.where(rt[:, k:k + 1] == lane, cf[:, k:k + 1], 0.0)
    dense = jnp.concatenate([dense, jnp.zeros((128 - TOK, 128), F32)], axis=0).astype(BF16)
    r16, l16 = iota((16, 128), 0), iota((16, 128), 1)
    r128, l128 = iota((128, 128), 0), iota((128, 128), 1)
    even = dot((l16 == 2 * r16).astype(BF16), dense, NT)
    odd = dot((l16 == 2 * r16 + 1).astype(BF16), dense, NT).astype(BF16)
    odd = dot(odd, (l128 == r128 + TOK).astype(BF16))
    ZR[0, 0, pl.ds(400, 16), :] = (even + odd).astype(BF16)

    pick = lane == core * TOK + iota((TOK, 128), 0)

    def ag(p, k, j):
        rows = pl.ds(0, AG_ROWS[j])
        if p:
            src, dst = lax.rem(13 - k, NZ), NZ - k
        else:
            src, dst = k - 1, k
        return remote(
            ZR.at[src, j, rows], ZR.at[dst, j, rows],
            ag_send.at[p, k - 1, j], zr_recv.at[dst, j], zdev(1 if p else -1),
        )

    def share(r, j):
        rows = pl.ds(0, AG_ROWS[j])
        return remote(ZR.at[r, j, rows], ZS.at[r, j, rows], sf_send.at[r, j], zs_recv.at[r, j], sib)

    def give(r, j):
        rows = pl.ds(0, RS_ROWS[j])
        return remote(SND.at[r, j, rows], SIB.at[r, j, rows], snd_send.at[r, j], sib_recv.at[r, j], sib)

    def rs(p, k, j):
        rows = pl.ds(0, RS_ROWS[j])
        src = k if p else NZ - k
        land = RP if p else RM
        return remote(
            OWN.at[src, j, rows], land.at[k - 1, j, rows],
            rs_send.at[p, k - 1, j], rs_recv.at[p, k - 1, j], zdev(1 if p else -1),
        )

    pl.semaphore_wait(barrier, 7)

    for p, j in ((1, 0), (0, 1), (1, 1), (0, 0)):
        ag(p, 1, j).start()
    share(0, 0).start()
    share(0, 1).start()
    load_g.wait()
    load_u.wait()

    def rows_of(ref, slots, j, lo):
        top, low = [], []
        for r in slots:
            for buf in (ZR, ZS):
                block = buf[r, j, pl.ds(lo, 80), :].astype(F32)
                top.append(block[:TOK])
                low.append(block[TOK:])
        return jnp.concatenate(top, axis=0), jnp.concatenate(low, axis=0)

    def first(slots, row0):
        n = 80 * len(slots)
        rows = pl.ds(row0, n)
        for r in slots:
            for j in range(2):
                share(r, j).wait_recv()
        for j in range(2):
            for b in range(4):
                top, low = rows_of(None, slots, j, 80 * b)
                X[rows, pl.ds(j * 512 + b * 128, 128)] = top.astype(BF16)
                X[rows, pl.ds(1024 + j * 512 + b * 128, 128)] = low.astype(BF16)
        g0 = rows_of(None, slots, 0, 320)
        g1 = rows_of(None, slots, 1, 320)
        weights = []
        for r in slots:
            for buf in (ZR, ZS):
                tile = buf[r, 0, pl.ds(400, 16), :].astype(F32)
                line = jnp.sum(jnp.where(r16 == z, tile, 0.0), axis=0, keepdims=True)
                weights.append(jnp.sum(jnp.where(pick, line, 0.0), axis=1, keepdims=True))
        weight = jnp.concatenate(weights, axis=0)
        total = jnp.zeros((n, 1), F32)
        for t in range(2):
            cot = jnp.concatenate([g0[t], g1[t]], axis=1)
            xs = X[rows, :]
            gate = dot(xs, WC[:, pl.ds(256 * t, 256)])
            up = dot(xs, WC[:, pl.ds(FF + 256 * t, 256)])
            sig = 1.0 / (1.0 + jnp.exp(-gate))
            act = gate * sig
            total = total + jnp.sum(act * up * cot, axis=1, keepdims=True)
            ups = weight * cot
            GU[rows, pl.ds(256 * t, 256)] = (
                ups * up * sig * (1.0 + gate * (1.0 - sig))
            ).astype(BF16)
            GU[rows, pl.ds(FF + 256 * t, 256)] = (ups * act).astype(BF16)
        i = 0
        for r in slots:
            for buf in (OWN, SND):
                line = jnp.sum(
                    jnp.where(pick, total[TOK * i:TOK * i + TOK], 0.0), axis=0, keepdims=True
                )
                buf[r, 0, pl.ds(320, 16), :] = jnp.where(r16 == z, line, 0.0).astype(BF16)
                i += 1

    def second(slots, row0):
        n = 80 * len(slots)
        grads = GU[pl.ds(row0, n), :]
        for j in range(2):
            top = dot(grads, WC[pl.ds(j * 512, 512), :], NT)
            low = dot(grads, WC[pl.ds(1024 + j * 512, 512), :], NT)
            i = 0
            for r in slots:
                for buf in (OWN, SND):
                    for b in range(4):
                        buf[r, j, pl.ds(80 * b, 80), :] = jnp.concatenate(
                            [
                                top[TOK * i:TOK * i + TOK, 128 * b:128 * b + 128],
                                low[TOK * i:TOK * i + TOK, 128 * b:128 * b + 128],
                            ],
                            axis=0,
                        ).astype(BF16)
                    i += 1
                give(r, j).start()

    def arrive(k, stage):
        for p in (1, 0):
            j = stage if p else 1 - stage
            ag(p, k, j).wait_recv()
            if stage == 0:
                ag(p, k + 1, j).start()
            else:
                @pl.when(k < 5)
                def _():
                    ag(p, k + 1, j).start()
            share(NZ - k if p else k, j).start()

    one, zero = jnp.int32(1), jnp.int32(0)
    arrive(1, 0)
    first([0], 0)
    arrive(1, 1)
    second([0], 0)

    def gather_step(k, carry):
        row0 = pl.multiple_of(80 + 160 * (k - 2), 16)
        arrive(k, 0)
        first([NZ + 1 - k, k - 1], row0)
        arrive(k, 1)
        second([NZ + 1 - k, k - 1], row0)
        return carry

    lax.fori_loop(2, 6, gather_step, 0)
    first([7, 5], 720)
    for p in (1, 0):
        j = 0 if p else 1
        ag(p, 6, j).wait_recv()
        share(6, j).start()
    first([6], 880)

    def weight_rows(dy):
        col = pl.multiple_of(lax.rem(y + dy, NY) * 256, 256)
        xs = X[:, pl.ds(col, 256)]
        PA[dy] = dot(xs, GU[:, pl.ds(0, CA)], TN).astype(BF16)
        PB[dy] = dot(xs, GU[:, pl.ds(CA, CB)], TN).astype(BF16)

    def xrow(step):
        return lax.rem(x + step, NX) * 64

    def near(p):
        return 1 if p else NX - 1

    def ax1(p, dy):
        row = pl.multiple_of(xrow(2) + (0 if p else 32), 32)
        return remote(
            PA.at[dy, pl.ds(row, 32)], AX1.at[p, dy], ax1_send.at[p, dy], ax1_recv.at[p, dy],
            xdev(1 if p else -1),
        )

    def ax2(p, dy):
        row = pl.multiple_of(xrow(near(p)), 64)
        return remote(
            PA.at[dy, pl.ds(row, 64)], AX2.at[p, dy], ax2_send.at[p, dy], ax2_recv.at[p, dy],
            xdev(1 if p else -1),
        )

    def a_open(dy):
        weight_rows(dy)
        ax1(1, dy).start()
        ax1(0, dy).start()

    def a_pass(dy):
        for p in (1, 0):
            ax1(p, dy).wait_recv()
            row = pl.multiple_of(xrow(near(p)) + (0 if p else 32), 32)
            PA[dy, pl.ds(row, 32), :] = (
                PA[dy, pl.ds(row, 32), :].astype(F32) + AX1[p, dy].astype(F32)
            ).astype(BF16)
            ax2(p, dy).start()

    def a_sum(dy):
        ax2(1, dy).wait_recv()
        ax2(0, dy).wait_recv()
        row = pl.multiple_of(x * 64, 64)
        SA[dy] = (
            PA[dy, pl.ds(row, 64), :].astype(F32)
            + AX2[1, dy].astype(F32) + AX2[0, dy].astype(F32)
        )

    def ay1(p):
        return remote(
            SAB.at[4, pl.ds(0 if p else 32, 32)], AY1.at[p], ay_send.at[p, 3], ay_recv.at[p, 3],
            ydev(1 if p else -1),
        )

    def ay(p, k):
        return remote(
            SAB.at[k if p else NY - k], AY.at[p, k - 1], ay_send.at[p, k - 1],
            ay_recv.at[p, k - 1], ydev(1 if p else -1),
        )

    def ay_first():
        SAB[4] = SA[4].astype(BF16)
        ay1(1).start()
        ay1(0).start()

    def ay_pass(k):
        for p in (1, 0):
            dy = k if p else NY - k
            if k == 3:
                ay1(p).wait_recv()
                lo = 0 if p else 32
                SAB[dy, pl.ds(32 - lo, 32), :] = SA[dy, pl.ds(32 - lo, 32), :].astype(BF16)
                SAB[dy, pl.ds(lo, 32), :] = (
                    SA[dy, pl.ds(lo, 32), :] + AY1[p].astype(F32)
                ).astype(BF16)
            else:
                ay(p, k + 1).wait_recv()
                SAB[dy] = (SA[dy] + AY[p, k].astype(F32)).astype(BF16)
            ay(p, k).start()

    def by(p, k, s):
        dy = k if p else NY - k
        return remote(
            PB.at[dy, pl.ds(128 * s, 128)], BY.at[p, k - 1, s], by_send.at[p, k - 1, s],
            by_recv.at[p, k - 1, s], ydev(1 if p else -1),
        )

    def b_pass(p, k, s):
        by(p, k + 1, s).wait_recv()
        dy = k if p else NY - k
        rows = pl.ds(128 * s, 128)
        PB[dy, rows, :] = (PB[dy, rows, :].astype(F32) + BY[p, k, s].astype(F32)).astype(BF16)
        by(p, k, s).start()

    def b_sum():
        for s in (1, 0):
            by(1, 1, s).wait_recv()
            by(0, 1, s).wait_recv()
            rows = pl.ds(128 * s, 128)
            SB[rows, :] = (
                PB[0, rows, :].astype(F32) + BY[1, 0, s].astype(F32) + BY[0, 0, s].astype(F32)
            )
        row = pl.multiple_of(xrow(2), 64)
        SBB[...] = SB[pl.ds(row, 64), :].astype(BF16)

    def bx1(p):
        return remote(
            SBB.at[pl.ds(0 if p else 32, 32)], BX1.at[p], bx1_send.at[p], bx1_recv.at[p],
            xdev(1 if p else -1),
        )

    def bx2(p):
        return remote(
            BXS.at[p], BX2.at[p], bx2_send.at[p], bx2_recv.at[p], xdev(1 if p else -1)
        )

    def bx_pass():
        for p in (1, 0):
            row = pl.multiple_of(xrow(near(p)), 64)
            mine = SB[pl.ds(row, 64), :]
            bx1(p).wait_recv()
            lo = 0 if p else 32
            BXS[p, pl.ds(32 - lo, 32), :] = mine[32 - lo:64 - lo].astype(BF16)
            BXS[p, pl.ds(lo, 32), :] = (mine[lo:lo + 32] + BX1[p].astype(F32)).astype(BF16)
            bx2(p).start()

    def mix(r, j):
        rows = pl.ds(0, RS_ROWS[j])
        return OWN[r, j, rows, :].astype(F32) + SIB[r, j, rows, :].astype(F32)

    def z_pass(p, k, j):
        r = k if p else NZ - k
        rows = pl.ds(0, RS_ROWS[j])
        give(r, j).wait_recv()
        total = mix(r, j)
        if k < 5 or (k == 5 and j == 1 - p):
            rs(p, k + 1, j).wait_recv()
            land = RP if p else RM
            total = total + land[k, j, rows, :].astype(F32)
        OWN[r, j, rows, :] = total.astype(BF16)
        rs(p, k, j).start()

    def z_step(k):
        for p, j in ((1, 1), (0, 0), (1, 0), (0, 1)):
            z_pass(p, k, j)

    a_open(4)
    by(1, 4, 0).start()
    by(0, 4, 1).start()
    second([7, 5, 6], 720)
    a_open(3)
    by(1, 3, 1).start()
    a_open(5)
    by(0, 3, 0).start()
    z_pass(1, 6, 0)
    z_pass(0, 6, 1)
    z_pass(1, 5, 1)
    z_pass(0, 5, 0)
    a_pass(4)
    b_pass(1, 3, 0)
    b_pass(0, 3, 1)
    a_open(2)
    a_open(6)
    z_pass(1, 5, 0)
    z_pass(0, 5, 1)
    a_pass(3)
    a_pass(5)
    a_sum(4)
    ay_first()
    for p, s in ((1, 1), (0, 0), (1, 0), (0, 1)):
        b_pass(p, 2, s)
    a_open(1)
    a_open(7)
    z_step(4)
    a_pass(2)
    a_pass(6)
    a_sum(3)
    a_sum(5)
    ay_pass(3)
    a_open(0)
    for p, s in ((1, 1), (0, 0), (1, 0), (0, 1)):
        b_pass(p, 1, s)
    z_step(3)
    a_pass(1)
    a_pass(7)
    a_sum(2)
    a_sum(6)
    ay_pass(2)
    b_sum()
    bx1(1).start()
    bx1(0).start()
    z_step(2)
    a_pass(0)
    a_sum(1)
    a_sum(7)
    ay_pass(1)
    bx_pass()
    z_step(1)

    a_sum(0)
    bx2(1).wait_recv()
    bx2(0).wait_recv()
    row = pl.multiple_of(x * 64, 64)
    du[:, pl.ds(CA - FF, CB)] = (
        SB[pl.ds(row, 64), :] + BX2[1].astype(F32) + BX2[0].astype(F32)
    )

    for j in (1, 0):
        rows = pl.ds(0, RS_ROWS[j])
        give(0, j).wait_recv()
        rs(1, 1, j).wait_recv()
        rs(0, 1, j).wait_recv()
        total = mix(0, j) + RP[0, j, rows, :].astype(F32) + RM[0, j, rows, :].astype(F32)
        for b in range(4):
            lo = j * 512 + b * 128
            gt[:, pl.ds(lo, 128)] = total[80 * b:80 * b + TOK].astype(BF16)
            gt[:, pl.ds(1024 + lo, 128)] = total[80 * b + TOK:80 * b + 80].astype(BF16)
        if j == 0:
            back = jnp.concatenate([total[320:336], jnp.zeros((112, 128), F32)], axis=0).astype(BF16)
            spread = jnp.zeros((TOK, 128), F32)
            for c in range(2):
                line = dot(
                    (lane == iota((TOK, 128), 0) + c * TOK).astype(BF16), back, NT
                ).astype(BF16)
                spread = spread + dot(line, (l128 == 2 * r128 + c).astype(BF16))
            out = jnp.zeros((TOK, 8), F32)
            lane8 = iota((TOK, 8), 1)
            for k in range(8):
                value = jnp.sum(
                    jnp.where(rt[:, k:k + 1] == lane, spread, 0.0), axis=1, keepdims=True
                )
                out = out + jnp.where(lane8 == k, value, 0.0)
            gc[...] = out.astype(BF16)

    ay(1, 1).wait_recv()
    ay(0, 1).wait_recv()
    total = SA[0] + AY[1, 0].astype(F32) + AY[0, 0].astype(F32)
    dg[...] = total[:, :FF]
    du[:, pl.ds(0, CA - FF)] = total[:, FF:]

    for p in (1, 0):
        for k in range(1, 7):
            for j in range(2):
                if k < 6 or j == 1 - p:
                    ag(p, k, j).wait_send()
                    rs(p, k, j).wait_send()
        for dy in range(NY):
            ax1(p, dy).wait_send()
            ax2(p, dy).wait_send()
        ay1(p).wait_send()
        for k in range(1, 4):
            ay(p, k).wait_send()
            for s in range(2):
                by(p, k, s).wait_send()
        by(p, 4, 1 - p).wait_send()
        bx1(p).wait_send()
        bx2(p).wait_send()
    for r in range(NZ):
        for j in range(2):
            share(r, j).wait_send()
            give(r, j).wait_send()


def per_device(tokens, grad_out, routes, combine, w_gate, w_up):
    vm = pl.BlockSpec(memory_space=pltpu.VMEM)
    hbm = pl.BlockSpec(memory_space=pl.ANY)
    V = pltpu.VMEM
    S = pltpu.SemaphoreType.DMA
    out = pl.pallas_call(
        kernel,
        out_shape=(
            jax.ShapeDtypeStruct((TOK, DM), BF16),
            jax.ShapeDtypeStruct((TOK, 8), BF16),
            jax.ShapeDtypeStruct((64, FF), F32),
            jax.ShapeDtypeStruct((64, FF), F32),
        ),
        in_specs=[vm, vm, vm, vm, hbm, hbm],
        out_specs=(vm, vm, vm, vm),
        scratch_shapes=[
            V((NZ, 2, 416, 128), BF16),
            V((NZ, 2, 416, 128), BF16),
            V((NZ * 80, DM), BF16),
            V((NZ * 80, 2 * FF), BF16),
            V((DM, 2 * FF), BF16),
            V((NZ, 2, 336, 128), BF16),
            V((NZ, 2, 336, 128), BF16),
            V((NZ, 2, 336, 128), BF16),
            V((6, 2, 336, 128), BF16),
            V((6, 2, 336, 128), BF16),
            V((NY, 256, CA), BF16),
            V((NY, 256, CB), BF16),
            V((2, NY, 32, CA), BF16),
            V((2, NY, 64, CA), BF16),
            V((NY, 64, CA), F32),
            V((NY, 64, CA), BF16),
            V((2, 32, CA), BF16),
            V((2, 3, 64, CA), BF16),
            V((2, 4, 2, 128, CB), BF16),
            V((256, CB), F32),
            V((64, CB), BF16),
            V((2, 32, CB), BF16),
            V((2, 64, CB), BF16),
            V((2, 64, CB), BF16),
            S((2,)),
            S((2, 6, 2)), S((NZ, 2)), S((NZ, 2)), S((NZ, 2)), S((NZ, 2)), S((NZ, 2)),
            S((2, 6, 2)), S((2, 6, 2)),
            S((2, NY)), S((2, NY)), S((2, NY)), S((2, NY)), S((2, 4)), S((2, 4)),
            S((2, 4, 2)), S((2, 4, 2)),
            S((2,)), S((2,)), S((2,)), S((2,)),
        ],
        compiler_params=pltpu.CompilerParams(
            collective_id=0, has_side_effects=True, vmem_limit_bytes=56 * 2**20
        ),
    )(tokens, grad_out, routes, combine, w_gate, w_up)
    return out[0], out[1], out[2][None], out[3][None]


def solution(mesh):
    return jax.shard_map(
        per_device,
        mesh=mesh,
        in_specs=(
            P(("dp", "expert"), None),
            P(("dp", "expert"), None),
            P(("dp", "expert"), None),
            P(("dp", "expert"), None),
            P("expert", None, None),
            P("expert", None, None),
        ),
        out_specs=(
            P(("dp", "expert"), None),
            P(("dp", "expert"), None),
            P("expert", "dp", None),
            P("expert", "dp", None),
        ),
        check_vma=False,
    )
```

```python
import functools

import jax
import jax.numpy as jnp
from jax import lax
from jax.experimental import pallas as pl
from jax.experimental.pallas import tpu as pltpu
from jax.sharding import PartitionSpec as P

F32 = jnp.float32
BF16 = jnp.bfloat16
MESH = pl.DeviceIdType.MESH

NX, NY, NZ = 4, 8, 12
TOK = 40
DM = 2048
FF = 512
AG_ROWS = (416, 400)
RS_ROWS = (336, 320)
CA = 640
CB = 2 * FF - CA
ORDER = (
    ("F6",), ("W", 4), ("BY", 1, 4, 0), ("BY", 0, 4, 1), ("S6",), ("W", 3), ("W", 5),
    ("A2", 1, 4), ("A2", 0, 4), ("BY", 1, 3, 1), ("BY", 0, 3, 0), ("Z", 1, 6, 1), ("Z", 1, 6, 0),
    ("Z", 0, 6, 2), ("Z", 0, 6, 3), ("BY", 1, 3, 0), ("BY", 0, 3, 1), ("W", 2), ("W", 6),
    ("A2", 1, 3), ("A2", 0, 3), ("A2", 1, 5), ("A2", 0, 5), ("Z", 1, 5, 1), ("Z", 0, 5, 1),
    ("Z", 1, 5, 0), ("Z", 1, 5, 2), ("Z", 1, 5, 3), ("Z", 0, 5, 0), ("Z", 0, 5, 2),
    ("Z", 0, 5, 3), ("A3", 4), ("BY", 1, 2, 1), ("BY", 0, 2, 0), ("W", 1), ("BY", 1, 2, 0),
    ("BY", 0, 2, 1), ("Z", 1, 4, 1), ("Z", 0, 4, 1), ("W", 7), ("Z", 1, 4, 0), ("Z", 0, 4, 0),
    ("A3", 3), ("Z", 1, 4, 2), ("Z", 0, 4, 2), ("A2", 1, 2), ("A2", 0, 2), ("A2", 1, 6),
    ("A2", 0, 6), ("Z", 1, 4, 3), ("Z", 0, 4, 3), ("A3", 5), ("AY", 1, 3), ("AY", 0, 3),
    ("BY", 1, 1, 1), ("BY", 0, 1, 0), ("Z", 1, 3, 1), ("Z", 0, 3, 1), ("W", 0), ("Z", 1, 3, 0),
    ("Z", 0, 3, 0), ("BY", 1, 1, 0), ("BY", 0, 1, 1), ("Z", 1, 3, 2), ("Z", 0, 3, 2),
    ("A2", 1, 1), ("A2", 0, 1), ("A3", 2), ("Z", 1, 3, 3), ("Z", 0, 3, 3), ("A2", 1, 7),
    ("A2", 0, 7), ("AY", 1, 2), ("Z", 1, 2, 1), ("Z", 0, 2, 1), ("A3", 6), ("AY", 0, 2),
    ("Z", 1, 2, 0), ("Z", 0, 2, 0), ("A2", 1, 0), ("A2", 0, 0), ("Z", 1, 2, 2), ("Z", 0, 2, 2),
    ("Z", 1, 2, 3), ("Z", 0, 2, 3), ("A3", 1), ("Z", 1, 1, 1), ("Z", 0, 1, 1), ("BS",),
    ("Z", 1, 1, 0), ("Z", 0, 1, 0), ("A3", 7), ("Z", 1, 1, 2), ("Z", 0, 1, 2), ("AY", 1, 1),
    ("AY", 0, 1), ("Z", 1, 1, 3), ("Z", 0, 1, 3), ("A3", 0), ("BX", 1), ("BX", 0), ("ZF", 1),
    ("ZF", 0), ("ZF", 2), ("AF",), ("ZF", 3), ("BF",),
)
NT = (((1,), (1,)), ((), ()))
TN = (((0,), (0,)), ((), ()))


def dot(a, b, dims=(((1,), (0,)), ((), ()))):
    return lax.dot_general(a, b, dims, preferred_element_type=F32)


def iota(shape, dim):
    return lax.broadcasted_iota(jnp.int32, shape, dim)


def kernel(
    tok_in, go_in, routes_in, comb_in, wg, wu,
    gt_out, gc_out, dg_out, du_out,
    tok, go, routes, comb, gt, gc, dg, du,
    ZR, ZS, X, GU, WC, OWN, SND, SIB, RP, RM,
    PA, PB, AX1, AX2, SA, SAB, AY1, AY, BY, SB, SBB, BX1, BX2, BXS,
    w_sem, in_sem, out_sem,
    ag_send, zr_recv, sf_send, zs_recv, snd_send, sib_recv, rs_send, rs_recv,
    ax1_send, ax1_recv, ax2_send, ax2_recv, ay_send, ay_recv, by_send, by_recv,
    bx1_send, bx1_recv, bx2_send, bx2_recv,
):
    dp = lax.axis_index("dp")
    ex = lax.axis_index("expert")
    x, y = lax.rem(dp, NX), dp // NX
    core, z = lax.rem(ex, 2), ex // 2

    def xdev(step):
        return (y * NX + lax.rem(x + step + NX, NX), ex)

    def ydev(step):
        return (lax.rem(y + step + NY, NY) * NX + x, ex)

    def zdev(step):
        return (dp, lax.rem(z + step + NZ, NZ) * 2 + core)

    sib = (dp, z * 2 + 1 - core)

    def remote(src, dst, ssem, rsem, dev):
        return pltpu.make_async_remote_copy(
            src_ref=src, dst_ref=dst, send_sem=ssem, recv_sem=rsem,
            device_id=dev, device_id_type=MESH,
        )

    barrier = pltpu.get_barrier_semaphore()
    for dev in (zdev(1), zdev(-1), sib, xdev(1), xdev(-1), ydev(1), ydev(-1)):
        pl.semaphore_signal(barrier, inc=1, device_id=dev, device_id_type=MESH)

    loads = [
        pltpu.make_async_copy(src, dst, in_sem.at[i])
        for i, (src, dst) in enumerate(
            ((tok_in, tok), (go_in, go), (routes_in, routes), (comb_in, comb))
        )
    ]
    stores = [
        pltpu.make_async_copy(src, dst, out_sem.at[i])
        for i, (src, dst) in enumerate(((gt, gt_out), (gc, gc_out), (dg, dg_out), (du, du_out)))
    ]
    load_g = pltpu.make_async_copy(wg.at[0], WC.at[:, pl.ds(0, FF)], w_sem.at[0])
    load_u = pltpu.make_async_copy(wu.at[0], WC.at[:, pl.ds(FF, FF)], w_sem.at[1])
    for load in loads:
        load.start()
    load_g.start()
    load_u.start()
    for load in loads:
        load.wait()

    tf = tok[...].astype(F32)
    gf = go[...].astype(F32)
    for j in range(2):
        for b in range(4):
            lo = j * 512 + b * 128
            ZR[0, j, pl.ds(80 * b, 80), :] = jnp.concatenate(
                [tf[:, lo:lo + 128], tf[:, 1024 + lo:1024 + lo + 128]], axis=0
            ).astype(BF16)
        ZR[0, j, pl.ds(320, 80), :] = jnp.concatenate(
            [gf[:, j * 128:j * 128 + 128], gf[:, 256 + j * 128:256 + j * 128 + 128]], axis=0
        ).astype(BF16)

    rt = routes[...]
    cf = comb[...].astype(F32)
    r16, r40 = iota((16, TOK), 0), iota((TOK, 128), 0)
    lane = iota((TOK, 128), 1)
    r16w = iota((16, 128), 0)
    spots = [(lane == r40 + c * TOK).astype(BF16) for c in range(2)]
    tile = jnp.zeros((16, 128), F32)
    for c in range(2):
        dense = jnp.zeros((16, TOK), F32)
        for k in range(8):
            dense = dense + jnp.where(rt[k:k + 1, :] == 2 * r16 + c, cf[k:k + 1, :], 0.0)
        tile = tile + dot(dense.astype(BF16), spots[c])
    ZR[0, 0, pl.ds(400, 16), :] = tile.astype(BF16)

    pick = lane == core * TOK + r40

    def ag(p, k, q):
        j, h = q // 2, q % 2
        rows = pl.ds(208 * h, AG_ROWS[j] - 208 if h else 208)
        if p:
            src, dst = lax.rem(13 - k, NZ), NZ - k
        else:
            src, dst = k - 1, k
        return remote(
            ZR.at[src, j, rows], ZR.at[dst, j, rows],
            ag_send.at[p, k - 1, q], zr_recv.at[dst, q], zdev(1 if p else -1),
        )

    def share(r, j):
        rows = pl.ds(0, AG_ROWS[j])
        return remote(ZR.at[r, j, rows], ZS.at[r, j, rows], sf_send.at[r, j], zs_recv.at[r, j], sib)

    def give(r, j):
        rows = pl.ds(0, RS_ROWS[j])
        return remote(SND.at[r, j, rows], SIB.at[r, j, rows], snd_send.at[r, j], sib_recv.at[r, j], sib)

    def part(q):
        return q // 2, pl.ds(160 * (q % 2), 176 if q == 1 else 160)

    def rs(p, k, q):
        j, rows = part(q)
        src = k if p else NZ - k
        land = RP if p else RM
        return remote(
            OWN.at[src, j, rows], land.at[k - 1, j, rows],
            rs_send.at[p, k - 1, q], rs_recv.at[p, k - 1, q], zdev(1 if p else -1),
        )

    pl.semaphore_wait(barrier, 7)

    for q in range(4):
        ag(1, 1, q).start()
        ag(0, 1, (q + 2) % 4).start()
    share(0, 0).start()
    share(0, 1).start()
    load_g.wait()
    load_u.wait()

    def rows_of(slots, j, lo):
        top, low = [], []
        for r in slots:
            for buf in (ZR, ZS):
                block = buf[r, j, pl.ds(lo, 80), :].astype(F32)
                top.append(block[:TOK])
                low.append(block[TOK:])
        return jnp.concatenate(top, axis=0), jnp.concatenate(low, axis=0)

    def gather_rows(slots, row0):
        n = 80 * len(slots)
        rows = pl.ds(row0, n)
        for r in slots:
            for j in range(2):
                share(r, j).wait_recv()
        for j in range(2):
            for b in range(4):
                top, low = rows_of(slots, j, 80 * b)
                X[rows, pl.ds(j * 512 + b * 128, 128)] = top.astype(BF16)
                X[rows, pl.ds(1024 + j * 512 + b * 128, 128)] = low.astype(BF16)
        weights = []
        for r in slots:
            for buf in (ZR, ZS):
                tile = buf[r, 0, pl.ds(400, 16), :].astype(F32)
                line = jnp.sum(jnp.where(r16w == z, tile, 0.0), axis=0, keepdims=True)
                weights.append(jnp.sum(jnp.where(pick, line, 0.0), axis=1, keepdims=True))
        return jnp.concatenate(weights, axis=0)

    def units(slots, row0, t, weight):
        rows = pl.ds(row0, 80 * len(slots))
        cot = jnp.concatenate([rows_of(slots, j, 320)[t] for j in range(2)], axis=1)
        xs = X[rows, :]
        gate = dot(xs, WC[:, pl.ds(256 * t, 256)])
        up = dot(xs, WC[:, pl.ds(FF + 256 * t, 256)])
        sig = 1.0 / (1.0 + jnp.exp(-gate))
        act = gate * sig
        ups = weight * cot
        GU[rows, pl.ds(256 * t, 256)] = (
            ups * up * sig * (1.0 + gate * (1.0 - sig))
        ).astype(BF16)
        GU[rows, pl.ds(FF + 256 * t, 256)] = (ups * act).astype(BF16)
        return jnp.sum(act * up * cot, axis=1, keepdims=True)

    def put_sums(slots, total):
        i = 0
        for r in slots:
            for buf in (OWN, SND):
                line = jnp.sum(
                    jnp.where(pick, total[TOK * i:TOK * i + TOK], 0.0), axis=0, keepdims=True
                )
                buf[r, 0, pl.ds(320, 16), :] = jnp.where(r16w == z, line, 0.0).astype(BF16)
                i += 1

    def first(slots, row0, between=None):
        weight = gather_rows(slots, row0)
        total = units(slots, row0, 0, weight)
        if between is not None:
            between()
        put_sums(slots, total + units(slots, row0, 1, weight))

    def second(slots, row0, j):
        grads = GU[pl.ds(row0, 80 * len(slots)), :]
        top = dot(grads, WC[pl.ds(j * 512, 512), :], NT)
        low = dot(grads, WC[pl.ds(1024 + j * 512, 512), :], NT)
        i = 0
        for r in slots:
            for buf in (OWN, SND):
                for b in range(4):
                    buf[r, j, pl.ds(80 * b, 80), :] = jnp.concatenate(
                        [
                            top[TOK * i:TOK * i + TOK, 128 * b:128 * b + 128],
                            low[TOK * i:TOK * i + TOK, 128 * b:128 * b + 128],
                        ],
                        axis=0,
                    ).astype(BF16)
                i += 1
            give(r, j).start()

    def arrive(k, i):
        for p in (1, 0):
            q = i if p else (i + 2) % 4
            ag(p, k, q).wait_recv()
            if i < 2:
                ag(p, k + 1, q).start()
            else:
                @pl.when(k < 5)
                def _():
                    ag(p, k + 1, q).start()
            if i % 2:
                share(NZ - k if p else k, q // 2).start()

    def pair(k):
        return [NZ - k, k], pl.multiple_of(160 * k - 80, 16)

    arrive(1, 0)
    arrive(1, 1)
    first([0], 0, lambda: arrive(1, 2))
    second([0], 0, 0)
    arrive(1, 3)
    second([0], 0, 1)

    def gather_step(k, carry, old=True):
        arrive(k, 0)
        if old:
            second(*pair(k - 2), 1)
        arrive(k, 1)
        first(*pair(k - 1), lambda: arrive(k, 2))
        arrive(k, 3)
        second(*pair(k - 1), 0)
        return carry

    gather_step(2, 0, False)
    lax.fori_loop(3, 6, gather_step, 0)
    for i in range(2):
        for p in (1, 0):
            ag(p, 6, i if p else i + 2).wait_recv()
            if i:
                share(6, 1 - p).start()
        if i == 0:
            second(*pair(4), 1)
    first(*pair(5))
    second(*pair(5), 0)
    second(*pair(5), 1)

    def weight_rows(dy):
        col = pl.multiple_of(lax.rem(y + dy, NY) * 256, 256)
        xs = X[:, pl.ds(col, 256)]
        PA[dy] = dot(xs, GU[:, pl.ds(0, CA)], TN).astype(BF16)
        PB[dy] = dot(xs, GU[:, pl.ds(CA, CB)], TN).astype(BF16)

    def xrow(step):
        return lax.rem(x + step, NX) * 64

    def near(p):
        return 1 if p else NX - 1

    def ax1(p, dy):
        row = pl.multiple_of(xrow(2) + (0 if p else 32), 32)
        return remote(
            PA.at[dy, pl.ds(row, 32)], AX1.at[p, dy], ax1_send.at[p, dy], ax1_recv.at[p, dy],
            xdev(1 if p else -1),
        )

    def ax2(p, dy):
        row = pl.multiple_of(xrow(near(p)), 64)
        return remote(
            PA.at[dy, pl.ds(row, 64)], AX2.at[p, dy], ax2_send.at[p, dy], ax2_recv.at[p, dy],
            xdev(1 if p else -1),
        )

    def a_open(dy):
        weight_rows(dy)
        ax1(1, dy).start()
        ax1(0, dy).start()

    def a_pass(p, dy):
        ax1(p, dy).wait_recv()
        row = pl.multiple_of(xrow(near(p)) + (0 if p else 32), 32)
        PA[dy, pl.ds(row, 32), :] = (
            PA[dy, pl.ds(row, 32), :].astype(F32) + AX1[p, dy].astype(F32)
        ).astype(BF16)
        ax2(p, dy).start()

    def a_sum(dy):
        ax2(1, dy).wait_recv()
        ax2(0, dy).wait_recv()
        row = pl.multiple_of(x * 64, 64)
        SA[dy] = (
            PA[dy, pl.ds(row, 64), :].astype(F32)
            + AX2[1, dy].astype(F32) + AX2[0, dy].astype(F32)
        )
        if dy == 4:
            SAB[4] = SA[4].astype(BF16)
            ay1(1).start()
            ay1(0).start()

    def ay1(p):
        return remote(
            SAB.at[4, pl.ds(0 if p else 32, 32)], AY1.at[p], ay_send.at[p, 3], ay_recv.at[p, 3],
            ydev(1 if p else -1),
        )

    def ay(p, k):
        return remote(
            SAB.at[k if p else NY - k], AY.at[p, k - 1], ay_send.at[p, k - 1],
            ay_recv.at[p, k - 1], ydev(1 if p else -1),
        )

    def ay_pass(p, k):
        dy = k if p else NY - k
        if k == 3:
            ay1(p).wait_recv()
            lo = 0 if p else 32
            SAB[dy, pl.ds(32 - lo, 32), :] = SA[dy, pl.ds(32 - lo, 32), :].astype(BF16)
            SAB[dy, pl.ds(lo, 32), :] = (
                SA[dy, pl.ds(lo, 32), :] + AY1[p].astype(F32)
            ).astype(BF16)
        else:
            ay(p, k + 1).wait_recv()
            SAB[dy] = (SA[dy] + AY[p, k].astype(F32)).astype(BF16)
        ay(p, k).start()

    def a_last():
        ay(1, 1).wait_recv()
        ay(0, 1).wait_recv()
        total = SA[0] + AY[1, 0].astype(F32) + AY[0, 0].astype(F32)
        dg[...] = total[:, :FF]
        du[:, pl.ds(0, CA - FF)] = total[:, FF:]
        stores[2].start()

    def by(p, k, s):
        dy = k if p else NY - k
        return remote(
            PB.at[dy, pl.ds(128 * s, 128)], BY.at[p, k - 1, s], by_send.at[p, k - 1, s],
            by_recv.at[p, k - 1, s], ydev(1 if p else -1),
        )

    def b_pass(p, k, s):
        dy = k if p else NY - k
        rows = pl.ds(128 * s, 128)
        if k < 3 or (k == 3 and s == 1 - p):
            by(p, k + 1, s).wait_recv()
            PB[dy, rows, :] = (PB[dy, rows, :].astype(F32) + BY[p, k, s].astype(F32)).astype(BF16)
        by(p, k, s).start()

    def b_sum():
        for s in (1, 0):
            by(1, 1, s).wait_recv()
            by(0, 1, s).wait_recv()
            rows = pl.ds(128 * s, 128)
            SB[rows, :] = (
                PB[0, rows, :].astype(F32) + BY[1, 0, s].astype(F32) + BY[0, 0, s].astype(F32)
            )
        row = pl.multiple_of(xrow(2), 64)
        SBB[...] = SB[pl.ds(row, 64), :].astype(BF16)
        bx1(1).start()
        bx1(0).start()

    def bx1(p):
        return remote(
            SBB.at[pl.ds(0 if p else 32, 32)], BX1.at[p], bx1_send.at[p], bx1_recv.at[p],
            xdev(1 if p else -1),
        )

    def bx2(p):
        return remote(
            BXS.at[p], BX2.at[p], bx2_send.at[p], bx2_recv.at[p], xdev(1 if p else -1)
        )

    def bx_pass(p):
        row = pl.multiple_of(xrow(near(p)), 64)
        mine = SB[pl.ds(row, 64), :]
        bx1(p).wait_recv()
        lo = 0 if p else 32
        BXS[p, pl.ds(32 - lo, 32), :] = mine[32 - lo:64 - lo].astype(BF16)
        BXS[p, pl.ds(lo, 32), :] = (mine[lo:lo + 32] + BX1[p].astype(F32)).astype(BF16)
        bx2(p).start()

    def b_last():
        bx2(1).wait_recv()
        bx2(0).wait_recv()
        row = pl.multiple_of(x * 64, 64)
        du[:, pl.ds(CA - FF, CB)] = (
            SB[pl.ds(row, 64), :] + BX2[1].astype(F32) + BX2[0].astype(F32)
        )

    given = set()

    def mix(r, q):
        j, rows = part(q)
        if (r, j) not in given:
            given.add((r, j))
            give(r, j).wait_recv()
        return OWN[r, j, rows, :].astype(F32) + SIB[r, j, rows, :].astype(F32)

    def z_pass(p, k, q):
        r = k if p else NZ - k
        j, rows = part(q)
        total = mix(r, q)
        if k < 5 or (k == 5 and j == 1 - p):
            rs(p, k + 1, q).wait_recv()
            land = RP if p else RM
            total = total + land[k, j, rows, :].astype(F32)
        OWN[r, j, rows, :] = total.astype(BF16)
        rs(p, k, q).start()

    def z_last(q):
        j, rows = part(q)
        rs(1, 1, q).wait_recv()
        rs(0, 1, q).wait_recv()
        total = mix(0, q) + RP[0, j, rows, :].astype(F32) + RM[0, j, rows, :].astype(F32)
        for b in range(2):
            lo = j * 512 + (q % 2 * 2 + b) * 128
            gt[:, pl.ds(lo, 128)] = total[80 * b:80 * b + TOK].astype(BF16)
            gt[:, pl.ds(1024 + lo, 128)] = total[80 * b + TOK:80 * b + 80].astype(BF16)
        if q == 1:
            back = total[160:176].astype(BF16)
            for k in range(8):
                gc[k:k + 1, :] = sum(
                    jnp.sum(
                        jnp.where(rt[k:k + 1, :] == 2 * r16 + c, dot(back, spots[c], NT), 0.0),
                        axis=0, keepdims=True,
                    )
                    for c in range(2)
                ).astype(BF16)
            stores[1].start()

    steps = {
        "F6": lambda: first([6], 880),
        "S6": lambda: [second([6], 880, j) for j in range(2)],
        "W": a_open, "A2": a_pass, "A3": a_sum, "AY": ay_pass, "AF": a_last,
        "BY": b_pass, "BS": b_sum, "BX": bx_pass, "BF": b_last,
        "Z": z_pass, "ZF": z_last,
    }
    for name, *where in ORDER:
        steps[name](*where)
    stores[0].start()
    stores[3].start()

    for p in (1, 0):
        for k in range(1, 7):
            for j in range(2):
                if k < 6 or j == 1 - p:
                    for q in (2 * j, 2 * j + 1):
                        ag(p, k, q).wait_send()
                        rs(p, k, q).wait_send()
        for dy in range(NY):
            ax1(p, dy).wait_send()
            ax2(p, dy).wait_send()
        ay1(p).wait_send()
        for k in range(1, 4):
            ay(p, k).wait_send()
            for s in range(2):
                by(p, k, s).wait_send()
        by(p, 4, 1 - p).wait_send()
        bx1(p).wait_send()
        bx2(p).wait_send()
    for r in range(NZ):
        for j in range(2):
            share(r, j).wait_send()
            give(r, j).wait_send()
    for store in stores:
        store.wait()


def hand_on(a, b, c, d, e, f, g, h, va, vb, vc, vd, sem, sem2):
    gets = [
        pltpu.make_async_copy(src, dst, sem.at[i])
        for i, (src, dst) in enumerate(((a, va), (b, vb), (c, vc), (d, vd)))
    ]
    puts = [
        pltpu.make_async_copy(src, dst, sem2.at[i])
        for i, (src, dst) in enumerate(((va, e), (vb, f), (vc, g), (vd, h)))
    ]
    for get in gets:
        get.start()
    for get, put in zip(gets, puts):
        get.wait()
        put.start()
    for put in puts:
        put.wait()


def per_device(tokens, grad_out, routes, combine, w_gate, w_up):
    hbm = pl.BlockSpec(memory_space=pl.ANY)
    V = pltpu.VMEM
    S = pltpu.SemaphoreType.DMA
    shapes = (
        jax.ShapeDtypeStruct((TOK, DM), BF16),
        jax.ShapeDtypeStruct((8, TOK), BF16),
        jax.ShapeDtypeStruct((64, FF), F32),
        jax.ShapeDtypeStruct((64, FF), F32),
    )
    out = pl.pallas_call(
        kernel,
        out_shape=shapes,
        in_specs=[hbm] * 6,
        out_specs=(hbm,) * 4,
        scratch_shapes=[
            V((TOK, DM), BF16),
            V((TOK, FF), BF16),
            V((8, TOK), jnp.int32),
            V((8, TOK), BF16),
            V((TOK, DM), BF16),
            V((8, TOK), BF16),
            V((64, FF), F32),
            V((64, FF), F32),
            V((NZ, 2, 416, 128), BF16),
            V((NZ, 2, 416, 128), BF16),
            V((NZ * 80, DM), BF16),
            V((NZ * 80, 2 * FF), BF16),
            V((DM, 2 * FF), BF16),
            V((NZ, 2, 336, 128), BF16),
            V((NZ, 2, 336, 128), BF16),
            V((NZ, 2, 336, 128), BF16),
            V((6, 2, 336, 128), BF16),
            V((6, 2, 336, 128), BF16),
            V((NY, 256, CA), BF16),
            V((NY, 256, CB), BF16),
            V((2, NY, 32, CA), BF16),
            V((2, NY, 64, CA), BF16),
            V((NY, 64, CA), F32),
            V((NY, 64, CA), BF16),
            V((2, 32, CA), BF16),
            V((2, 3, 64, CA), BF16),
            V((2, 4, 2, 128, CB), BF16),
            V((256, CB), F32),
            V((64, CB), BF16),
            V((2, 32, CB), BF16),
            V((2, 64, CB), BF16),
            V((2, 64, CB), BF16),
            S((2,)), S((4,)), S((4,)),
            S((2, 6, 4)), S((NZ, 4)), S((NZ, 2)), S((NZ, 2)), S((NZ, 2)), S((NZ, 2)),
            S((2, 6, 4)), S((2, 6, 4)),
            S((2, NY)), S((2, NY)), S((2, NY)), S((2, NY)), S((2, 4)), S((2, 4)),
            S((2, 4, 2)), S((2, 4, 2)),
            S((2,)), S((2,)), S((2,)), S((2,)),
        ],
        compiler_params=pltpu.CompilerParams(
            collective_id=0, has_side_effects=True, vmem_limit_bytes=56 * 2**20
        ),
    )(tokens, grad_out, routes.T, combine.T, w_gate, w_up)
    out = pl.pallas_call(
        hand_on,
        out_shape=shapes,
        in_specs=[hbm] * 4,
        out_specs=(hbm,) * 4,
        scratch_shapes=[V(x.shape, x.dtype) for x in shapes] + [S((4,)), S((4,))],
    )(*out)
    return out[0], out[1].T, out[2][None], out[3][None]


def solution(mesh):
    return jax.shard_map(
        per_device,
        mesh=mesh,
        in_specs=(
            P(("dp", "expert"), None),
            P(("dp", "expert"), None),
            P(("dp", "expert"), None),
            P(("dp", "expert"), None),
            P("expert", None, None),
            P("expert", None, None),
        ),
        out_specs=(
            P(("dp", "expert"), None),
            P(("dp", "expert"), None),
            P("expert", "dp", None),
            P("expert", "dp", None),
        ),
        check_vma=False,
    )
```

```python
import functools

import jax
import jax.numpy as jnp
from jax import lax
from jax.experimental import pallas as pl
from jax.experimental.pallas import tpu as pltpu
from jax.sharding import PartitionSpec as P

F32 = jnp.float32
BF16 = jnp.bfloat16
MESH = pl.DeviceIdType.MESH

NX, NY, NZ = 4, 8, 12
TOK = 40
DM = 2048
FF = 512
AG_ROWS = (416, 400)
RS_ROWS = (336, 320)
CA = 640
CB = 2 * FF - CA
ORDER = (
    ("F5",), ("S5", 1), ("F6",), ("W", 4), ("BY", 0, 4, 1), ("BY", 1, 4, 0), ("S6", 0), ("S6", 1),
    ("W", 3), ("BY", 1, 3, 1), ("W", 5), ("BY", 0, 3, 0), ("S5", 0), ("Z", 1, 6, 1), ("A2", 0, 4),
    ("A2", 1, 4), ("Z", 1, 6, 0), ("Z", 0, 6, 3), ("Z", 1, 5, 2), ("Z", 0, 6, 2), ("W", 2),
    ("BY", 1, 3, 0), ("BY", 0, 3, 1), ("Z", 1, 5, 3), ("A2", 0, 3), ("Z", 0, 5, 0), ("A2", 1, 5),
    ("Z", 0, 5, 1), ("W", 6), ("BY", 1, 2, 1), ("Z", 1, 5, 1), ("BY", 0, 2, 0), ("Z", 0, 5, 3),
    ("A2", 1, 3), ("A2", 0, 5), ("Z", 1, 5, 0), ("A3", 4), ("Z", 0, 5, 2), ("Z", 1, 4, 2),
    ("W", 1), ("Z", 0, 4, 0), ("BY", 1, 2, 0), ("A2", 1, 2), ("Z", 1, 4, 3), ("BY", 0, 2, 1),
    ("Z", 0, 4, 1), ("Z", 1, 4, 1), ("A2", 0, 2), ("Z", 0, 4, 3), ("W", 7), ("Z", 1, 4, 0),
    ("BY", 1, 1, 1), ("BY", 0, 1, 0), ("Z", 0, 4, 2), ("Z", 1, 3, 2), ("Z", 0, 3, 0), ("A3", 3),
    ("AY", 1, 3), ("A2", 0, 6), ("Z", 1, 3, 3), ("A2", 1, 6), ("Z", 0, 3, 1), ("A3", 5),
    ("A2", 1, 1), ("AY", 0, 3), ("Z", 1, 3, 1), ("Z", 0, 3, 3), ("W", 0), ("Z", 1, 3, 0),
    ("BY", 1, 1, 0), ("BY", 0, 1, 1), ("Z", 0, 3, 2), ("A2", 0, 1), ("A2", 1, 7), ("Z", 1, 2, 2),
    ("Z", 0, 2, 0), ("Z", 1, 2, 3), ("A3", 2), ("Z", 0, 2, 1), ("A2", 0, 7), ("A3", 6),
    ("Z", 1, 2, 1), ("AY", 1, 2), ("AY", 0, 2), ("Z", 0, 2, 3), ("Z", 1, 2, 0), ("Z", 0, 2, 2),
    ("Z", 1, 1, 2), ("Z", 0, 1, 0), ("BS",), ("Z", 1, 1, 3), ("A2", 0, 0), ("Z", 0, 1, 1),
    ("A3", 1), ("Z", 1, 1, 1), ("A2", 1, 0), ("A3", 7), ("AY", 1, 1), ("AY", 0, 1),
    ("Z", 0, 1, 3), ("Z", 1, 1, 0), ("Z", 0, 1, 2), ("BX", 1), ("BX", 0), ("ZF", 1), ("ZF", 3),
    ("A3", 0), ("ZF", 0), ("AF",), ("ZF", 2), ("BF",),
)
NT = (((1,), (1,)), ((), ()))
TN = (((0,), (0,)), ((), ()))


def dot(a, b, dims=(((1,), (0,)), ((), ()))):
    return lax.dot_general(a, b, dims, preferred_element_type=F32)


def iota(shape, dim):
    return lax.broadcasted_iota(jnp.int32, shape, dim)


def kernel(
    tok_in, go_in, routes_in, comb_in, wg, wu,
    gt_out, gc_out, dg_out, du_out,
    tok, go, routes, comb, gt, gc, dg, du,
    ZR, ZS, X, GU, WC, OWN, SND, SIB, RP, RM,
    PA, PB, AX1, AX2, SA, SAB, AY1, AY, BY, SB, SBB, BX1, BX2, BXS,
    w_sem, in_sem, out_sem,
    ag_send, zr_recv, sf_send, zs_recv, snd_send, sib_recv, rs_send, rs_recv,
    ax1_send, ax1_recv, ax2_send, ax2_recv, ay_send, ay_recv, by_send, by_recv,
    bx1_send, bx1_recv, bx2_send, bx2_recv,
):
    dp = lax.axis_index("dp")
    ex = lax.axis_index("expert")
    x, y = lax.rem(dp, NX), dp // NX
    core, z = lax.rem(ex, 2), ex // 2

    def xdev(step):
        return (y * NX + lax.rem(x + step + NX, NX), ex)

    def ydev(step):
        return (lax.rem(y + step + NY, NY) * NX + x, ex)

    def zdev(step):
        return (dp, lax.rem(z + step + NZ, NZ) * 2 + core)

    sib = (dp, z * 2 + 1 - core)

    def remote(src, dst, ssem, rsem, dev):
        return pltpu.make_async_remote_copy(
            src_ref=src, dst_ref=dst, send_sem=ssem, recv_sem=rsem,
            device_id=dev, device_id_type=MESH,
        )

    barrier = pltpu.get_barrier_semaphore()
    for dev in (zdev(1), zdev(-1), sib, xdev(1), xdev(-1), ydev(1), ydev(-1)):
        pl.semaphore_signal(barrier, inc=1, device_id=dev, device_id_type=MESH)

    loads = [
        pltpu.make_async_copy(src, dst, in_sem.at[i])
        for i, (src, dst) in enumerate(
            ((tok_in, tok), (go_in, go), (routes_in, routes), (comb_in, comb))
        )
    ]
    stores = [
        pltpu.make_async_copy(src, dst, out_sem.at[i])
        for i, (src, dst) in enumerate(((gt, gt_out), (gc, gc_out), (dg, dg_out), (du, du_out)))
    ]
    load_g = pltpu.make_async_copy(wg.at[0], WC.at[:, pl.ds(0, FF)], w_sem.at[0])
    load_u = pltpu.make_async_copy(wu.at[0], WC.at[:, pl.ds(FF, FF)], w_sem.at[1])
    for load in loads:
        load.start()
    load_g.start()
    load_u.start()
    for load in loads:
        load.wait()

    tf = tok[...].astype(F32)
    gf = go[...].astype(F32)
    for j in range(2):
        for b in range(4):
            lo = j * 512 + b * 128
            ZR[0, j, pl.ds(80 * b, 80), :] = jnp.concatenate(
                [tf[:, lo:lo + 128], tf[:, 1024 + lo:1024 + lo + 128]], axis=0
            ).astype(BF16)
        ZR[0, j, pl.ds(320, 80), :] = jnp.concatenate(
            [gf[:, j * 128:j * 128 + 128], gf[:, 256 + j * 128:256 + j * 128 + 128]], axis=0
        ).astype(BF16)

    def ag(p, k, q):
        j, h = q // 2, q % 2
        rows = pl.ds(208 * h, AG_ROWS[j] - 208 if h else 208)
        if p:
            src, dst = lax.rem(13 - k, NZ), NZ - k
        else:
            src, dst = k - 1, k
        return remote(
            ZR.at[src, j, rows], ZR.at[dst, j, rows],
            ag_send.at[p, k - 1, q], zr_recv.at[dst, q], zdev(1 if p else -1),
        )

    def share(r, j):
        rows = pl.ds(0, AG_ROWS[j])
        return remote(ZR.at[r, j, rows], ZS.at[r, j, rows], sf_send.at[r, j], zs_recv.at[r, j], sib)

    def give(r, j):
        rows = pl.ds(0, RS_ROWS[j])
        return remote(SND.at[r, j, rows], SIB.at[r, j, rows], snd_send.at[r, j], sib_recv.at[r, j], sib)

    def part(q):
        return q // 2, pl.ds(160 * (q % 2), 176 if q == 1 else 160)

    def rs(p, k, q):
        j, rows = part(q)
        src = k if p else NZ - k
        land = RP if p else RM
        return remote(
            OWN.at[src, j, rows], land.at[k - 1, j, rows],
            rs_send.at[p, k - 1, q], rs_recv.at[p, k - 1, q], zdev(1 if p else -1),
        )

    pl.semaphore_wait(barrier, 7)
    ag(1, 1, 0).start()
    ag(0, 1, 2).start()

    rt = routes[...]
    cf = comb[...].astype(F32)
    r16, r40 = iota((16, TOK), 0), iota((TOK, 128), 0)
    lane = iota((TOK, 128), 1)
    r16w = iota((16, 128), 0)
    spots = [(lane == r40 + c * TOK).astype(BF16) for c in range(2)]
    tile = jnp.zeros((16, 128), F32)
    for c in range(2):
        dense = jnp.zeros((16, TOK), F32)
        for k in range(8):
            dense = dense + jnp.where(rt[k:k + 1, :] == 2 * r16 + c, cf[k:k + 1, :], 0.0)
        tile = tile + dot(dense.astype(BF16), spots[c])
    ZR[0, 0, pl.ds(400, 16), :] = tile.astype(BF16)

    pick = lane == core * TOK + r40

    for q in range(1, 4):
        ag(1, 1, q).start()
        ag(0, 1, (q + 2) % 4).start()
    share(0, 0).start()
    share(0, 1).start()
    load_g.wait()
    load_u.wait()

    def rows_of(slots, j, lo):
        top, low = [], []
        for r in slots:
            for buf in (ZR, ZS):
                block = buf[r, j, pl.ds(lo, 80), :].astype(F32)
                top.append(block[:TOK])
                low.append(block[TOK:])
        return jnp.concatenate(top, axis=0), jnp.concatenate(low, axis=0)

    def gather_rows(slots, row0):
        n = 80 * len(slots)
        rows = pl.ds(row0, n)
        for r in slots:
            for j in range(2):
                share(r, j).wait_recv()
        for j in range(2):
            for b in range(4):
                top, low = rows_of(slots, j, 80 * b)
                X[rows, pl.ds(j * 512 + b * 128, 128)] = top.astype(BF16)
                X[rows, pl.ds(1024 + j * 512 + b * 128, 128)] = low.astype(BF16)
        weights = []
        for r in slots:
            for buf in (ZR, ZS):
                tile = buf[r, 0, pl.ds(400, 16), :].astype(F32)
                line = jnp.sum(jnp.where(r16w == z, tile, 0.0), axis=0, keepdims=True)
                weights.append(jnp.sum(jnp.where(pick, line, 0.0), axis=1, keepdims=True))
        return jnp.concatenate(weights, axis=0)

    def units(slots, row0, t, weight):
        rows = pl.ds(row0, 80 * len(slots))
        cot = jnp.concatenate([rows_of(slots, j, 320)[t] for j in range(2)], axis=1)
        xs = X[rows, :]
        gate = dot(xs, WC[:, pl.ds(256 * t, 256)])
        up = dot(xs, WC[:, pl.ds(FF + 256 * t, 256)])
        sig = 1.0 / (1.0 + jnp.exp(-gate))
        act = gate * sig
        ups = weight * cot
        GU[rows, pl.ds(256 * t, 256)] = (
            ups * up * sig * (1.0 + gate * (1.0 - sig))
        ).astype(BF16)
        GU[rows, pl.ds(FF + 256 * t, 256)] = (ups * act).astype(BF16)
        return jnp.sum(act * up * cot, axis=1, keepdims=True)

    def put_sums(slots, total):
        i = 0
        for r in slots:
            for buf in (OWN, SND):
                line = jnp.sum(
                    jnp.where(pick, total[TOK * i:TOK * i + TOK], 0.0), axis=0, keepdims=True
                )
                buf[r, 0, pl.ds(320, 16), :] = jnp.where(r16w == z, line, 0.0).astype(BF16)
                i += 1

    def first(slots, row0, between=None):
        weight = gather_rows(slots, row0)
        total = units(slots, row0, 0, weight)
        if between is not None:
            between()
        put_sums(slots, total + units(slots, row0, 1, weight))

    def second(slots, row0, j):
        grads = GU[pl.ds(row0, 80 * len(slots)), :]
        top = dot(grads, WC[pl.ds(j * 512, 512), :], NT)
        low = dot(grads, WC[pl.ds(1024 + j * 512, 512), :], NT)
        i = 0
        for r in slots:
            for buf in (OWN, SND):
                for b in range(4):
                    buf[r, j, pl.ds(80 * b, 80), :] = jnp.concatenate(
                        [
                            top[TOK * i:TOK * i + TOK, 128 * b:128 * b + 128],
                            low[TOK * i:TOK * i + TOK, 128 * b:128 * b + 128],
                        ],
                        axis=0,
                    ).astype(BF16)
                i += 1
            give(r, j).start()

    def arrive(k, i):
        for p in (1, 0):
            q = i if p else (i + 2) % 4
            ag(p, k, q).wait_recv()
            if i < 2:
                ag(p, k + 1, q).start()
            else:
                @pl.when(k < 5)
                def _():
                    ag(p, k + 1, q).start()
            if i % 2:
                share(NZ - k if p else k, q // 2).start()

    def pair(k):
        return [NZ - k, k], pl.multiple_of(160 * k - 80, 16)

    arrive(1, 0)
    arrive(1, 1)
    first([0], 0, lambda: arrive(1, 2))
    second([0], 0, 0)
    arrive(1, 3)
    second([0], 0, 1)

    def gather_step(k, carry, old=True):
        arrive(k, 0)
        if old:
            second(*pair(k - 2), 1)
        arrive(k, 1)
        first(*pair(k - 1), lambda: arrive(k, 2))
        arrive(k, 3)
        second(*pair(k - 1), 0)
        return carry

    gather_step(2, 0, False)
    lax.fori_loop(3, 6, gather_step, 0)
    for i in range(2):
        for p in (1, 0):
            ag(p, 6, i if p else i + 2).wait_recv()
            if i:
                share(6, 1 - p).start()
        if i == 0:
            second(*pair(4), 1)

    def weight_rows(dy):
        col = pl.multiple_of(lax.rem(y + dy, NY) * 256, 256)
        xs = X[:, pl.ds(col, 256)]
        PA[dy] = dot(xs, GU[:, pl.ds(0, CA)], TN).astype(BF16)
        PB[dy] = dot(xs, GU[:, pl.ds(CA, CB)], TN).astype(BF16)

    def xrow(step):
        return lax.rem(x + step, NX) * 64

    def near(p):
        return 1 if p else NX - 1

    def ax1(p, dy):
        row = pl.multiple_of(xrow(2) + (0 if p else 32), 32)
        return remote(
            PA.at[dy, pl.ds(row, 32)], AX1.at[p, dy], ax1_send.at[p, dy], ax1_recv.at[p, dy],
            xdev(1 if p else -1),
        )

    def ax2(p, dy):
        row = pl.multiple_of(xrow(near(p)), 64)
        return remote(
            PA.at[dy, pl.ds(row, 64)], AX2.at[p, dy], ax2_send.at[p, dy], ax2_recv.at[p, dy],
            xdev(1 if p else -1),
        )

    def a_open(dy):
        weight_rows(dy)
        ax1(1, dy).start()
        ax1(0, dy).start()

    def a_pass(p, dy):
        ax1(p, dy).wait_recv()
        row = pl.multiple_of(xrow(near(p)) + (0 if p else 32), 32)
        PA[dy, pl.ds(row, 32), :] = (
            PA[dy, pl.ds(row, 32), :].astype(F32) + AX1[p, dy].astype(F32)
        ).astype(BF16)
        ax2(p, dy).start()

    def a_sum(dy):
        ax2(1, dy).wait_recv()
        ax2(0, dy).wait_recv()
        row = pl.multiple_of(x * 64, 64)
        SA[dy] = (
            PA[dy, pl.ds(row, 64), :].astype(F32)
            + AX2[1, dy].astype(F32) + AX2[0, dy].astype(F32)
        )
        if dy == 4:
            SAB[4] = SA[4].astype(BF16)
            ay1(1).start()
            ay1(0).start()

    def ay1(p):
        return remote(
            SAB.at[4, pl.ds(0 if p else 32, 32)], AY1.at[p], ay_send.at[p, 3], ay_recv.at[p, 3],
            ydev(1 if p else -1),
        )

    def ay(p, k):
        return remote(
            SAB.at[k if p else NY - k], AY.at[p, k - 1], ay_send.at[p, k - 1],
            ay_recv.at[p, k - 1], ydev(1 if p else -1),
        )

    def ay_pass(p, k):
        dy = k if p else NY - k
        if k == 3:
            ay1(p).wait_recv()
            lo = 0 if p else 32
            SAB[dy, pl.ds(32 - lo, 32), :] = SA[dy, pl.ds(32 - lo, 32), :].astype(BF16)
            SAB[dy, pl.ds(lo, 32), :] = (
                SA[dy, pl.ds(lo, 32), :] + AY1[p].astype(F32)
            ).astype(BF16)
        else:
            ay(p, k + 1).wait_recv()
            SAB[dy] = (SA[dy] + AY[p, k].astype(F32)).astype(BF16)
        ay(p, k).start()

    def a_last():
        ay(1, 1).wait_recv()
        ay(0, 1).wait_recv()
        total = SA[0] + AY[1, 0].astype(F32) + AY[0, 0].astype(F32)
        dg[...] = total[:, :FF]
        du[:, pl.ds(0, CA - FF)] = total[:, FF:]
        stores[2].start()

    def by(p, k, s):
        dy = k if p else NY - k
        return remote(
            PB.at[dy, pl.ds(128 * s, 128)], BY.at[p, k - 1, s], by_send.at[p, k - 1, s],
            by_recv.at[p, k - 1, s], ydev(1 if p else -1),
        )

    def b_pass(p, k, s):
        dy = k if p else NY - k
        rows = pl.ds(128 * s, 128)
        if k < 3 or (k == 3 and s == 1 - p):
            by(p, k + 1, s).wait_recv()
            PB[dy, rows, :] = (PB[dy, rows, :].astype(F32) + BY[p, k, s].astype(F32)).astype(BF16)
        by(p, k, s).start()

    def b_sum():
        for s in (1, 0):
            by(1, 1, s).wait_recv()
            by(0, 1, s).wait_recv()
            rows = pl.ds(128 * s, 128)
            SB[rows, :] = (
                PB[0, rows, :].astype(F32) + BY[1, 0, s].astype(F32) + BY[0, 0, s].astype(F32)
            )
        row = pl.multiple_of(xrow(2), 64)
        SBB[...] = SB[pl.ds(row, 64), :].astype(BF16)
        bx1(1).start()
        bx1(0).start()

    def bx1(p):
        return remote(
            SBB.at[pl.ds(0 if p else 32, 32)], BX1.at[p], bx1_send.at[p], bx1_recv.at[p],
            xdev(1 if p else -1),
        )

    def bx2(p):
        return remote(
            BXS.at[p], BX2.at[p], bx2_send.at[p], bx2_recv.at[p], xdev(1 if p else -1)
        )

    def bx_pass(p):
        row = pl.multiple_of(xrow(near(p)), 64)
        mine = SB[pl.ds(row, 64), :]
        bx1(p).wait_recv()
        lo = 0 if p else 32
        BXS[p, pl.ds(32 - lo, 32), :] = mine[32 - lo:64 - lo].astype(BF16)
        BXS[p, pl.ds(lo, 32), :] = (mine[lo:lo + 32] + BX1[p].astype(F32)).astype(BF16)
        bx2(p).start()

    def b_last():
        bx2(1).wait_recv()
        bx2(0).wait_recv()
        row = pl.multiple_of(x * 64, 64)
        du[:, pl.ds(CA - FF, CB)] = (
            SB[pl.ds(row, 64), :] + BX2[1].astype(F32) + BX2[0].astype(F32)
        )

    given = set()

    def mix(r, q):
        j, rows = part(q)
        if (r, j) not in given:
            given.add((r, j))
            give(r, j).wait_recv()
        return OWN[r, j, rows, :].astype(F32) + SIB[r, j, rows, :].astype(F32)

    def z_pass(p, k, q):
        r = k if p else NZ - k
        j, rows = part(q)
        total = mix(r, q)
        if k < 5 or (k == 5 and j == 1 - p):
            rs(p, k + 1, q).wait_recv()
            land = RP if p else RM
            total = total + land[k, j, rows, :].astype(F32)
        OWN[r, j, rows, :] = total.astype(BF16)
        rs(p, k, q).start()

    def z_last(q):
        j, rows = part(q)
        rs(1, 1, q).wait_recv()
        rs(0, 1, q).wait_recv()
        total = mix(0, q) + RP[0, j, rows, :].astype(F32) + RM[0, j, rows, :].astype(F32)
        for b in range(2):
            lo = j * 512 + (q % 2 * 2 + b) * 128
            gt[:, pl.ds(lo, 128)] = total[80 * b:80 * b + TOK].astype(BF16)
            gt[:, pl.ds(1024 + lo, 128)] = total[80 * b + TOK:80 * b + 80].astype(BF16)
        if q == 1:
            back = total[160:176].astype(BF16)
            for k in range(8):
                gc[k:k + 1, :] = sum(
                    jnp.sum(
                        jnp.where(rt[k:k + 1, :] == 2 * r16 + c, dot(back, spots[c], NT), 0.0),
                        axis=0, keepdims=True,
                    )
                    for c in range(2)
                ).astype(BF16)
            stores[1].start()

    steps = {
        "F5": lambda: first(*pair(5)),
        "S5": lambda j: second(*pair(5), j),
        "F6": lambda: first([6], 880),
        "S6": lambda j: second([6], 880, j),
        "W": a_open, "A2": a_pass, "A3": a_sum, "AY": ay_pass, "AF": a_last,
        "BY": b_pass, "BS": b_sum, "BX": bx_pass, "BF": b_last,
        "Z": z_pass, "ZF": z_last,
    }
    for name, *where in ORDER:
        steps[name](*where)
    stores[0].start()
    stores[3].start()

    for p in (1, 0):
        for k in range(1, 7):
            for j in range(2):
                if k < 6 or j == 1 - p:
                    for q in (2 * j, 2 * j + 1):
                        ag(p, k, q).wait_send()
                        rs(p, k, q).wait_send()
        for dy in range(NY):
            ax1(p, dy).wait_send()
            ax2(p, dy).wait_send()
        ay1(p).wait_send()
        for k in range(1, 4):
            ay(p, k).wait_send()
            for s in range(2):
                by(p, k, s).wait_send()
        by(p, 4, 1 - p).wait_send()
        bx1(p).wait_send()
        bx2(p).wait_send()
    for r in range(NZ):
        for j in range(2):
            share(r, j).wait_send()
            give(r, j).wait_send()
    for store in stores:
        store.wait()


def hand_on(a, b, c, d, e, f, g, h, va, vb, vc, vd, sem, sem2):
    gets = [
        pltpu.make_async_copy(src, dst, sem.at[i])
        for i, (src, dst) in enumerate(((a, va), (b, vb), (c, vc), (d, vd)))
    ]
    puts = [
        pltpu.make_async_copy(src, dst, sem2.at[i])
        for i, (src, dst) in enumerate(((va, e), (vb, f), (vc, g), (vd, h)))
    ]
    for get in gets:
        get.start()
    for get, put in zip(gets, puts):
        get.wait()
        put.start()
    for put in puts:
        put.wait()


def per_device(tokens, grad_out, routes, combine, w_gate, w_up):
    hbm = pl.BlockSpec(memory_space=pl.ANY)
    V = pltpu.VMEM
    S = pltpu.SemaphoreType.DMA
    shapes = (
        jax.ShapeDtypeStruct((TOK, DM), BF16),
        jax.ShapeDtypeStruct((8, TOK), BF16),
        jax.ShapeDtypeStruct((64, FF), F32),
        jax.ShapeDtypeStruct((64, FF), F32),
    )
    out = pl.pallas_call(
        kernel,
        out_shape=shapes,
        in_specs=[pl.BlockSpec(memory_space=pltpu.HBM)] * 6,
        out_specs=(hbm,) * 4,
        scratch_shapes=[
            V((TOK, DM), BF16),
            V((TOK, FF), BF16),
            V((8, TOK), jnp.int32),
            V((8, TOK), BF16),
            V((TOK, DM), BF16),
            V((8, TOK), BF16),
            V((64, FF), F32),
            V((64, FF), F32),
            V((NZ, 2, 416, 128), BF16),
            V((NZ, 2, 416, 128), BF16),
            V((NZ * 80, DM), BF16),
            V((NZ * 80, 2 * FF), BF16),
            V((DM, 2 * FF), BF16),
            V((NZ, 2, 336, 128), BF16),
            V((NZ, 2, 336, 128), BF16),
            V((NZ, 2, 336, 128), BF16),
            V((6, 2, 336, 128), BF16),
            V((6, 2, 336, 128), BF16),
            V((NY, 256, CA), BF16),
            V((NY, 256, CB), BF16),
            V((2, NY, 32, CA), BF16),
            V((2, NY, 64, CA), BF16),
            V((NY, 64, CA), F32),
            V((NY, 64, CA), BF16),
            V((2, 32, CA), BF16),
            V((2, 3, 64, CA), BF16),
            V((2, 4, 2, 128, CB), BF16),
            V((256, CB), F32),
            V((64, CB), BF16),
            V((2, 32, CB), BF16),
            V((2, 64, CB), BF16),
            V((2, 64, CB), BF16),
            S((2,)), S((4,)), S((4,)),
            S((2, 6, 4)), S((NZ, 4)), S((NZ, 2)), S((NZ, 2)), S((NZ, 2)), S((NZ, 2)),
            S((2, 6, 4)), S((2, 6, 4)),
            S((2, NY)), S((2, NY)), S((2, NY)), S((2, NY)), S((2, 4)), S((2, 4)),
            S((2, 4, 2)), S((2, 4, 2)),
            S((2,)), S((2,)), S((2,)), S((2,)),
        ],
        compiler_params=pltpu.CompilerParams(
            collective_id=0, has_side_effects=True, vmem_limit_bytes=56 * 2**20
        ),
    )(tokens, grad_out, routes.T, combine.T, w_gate, w_up)
    out = pl.pallas_call(
        hand_on,
        out_shape=shapes,
        in_specs=[hbm] * 4,
        out_specs=(hbm,) * 4,
        scratch_shapes=[V(x.shape, x.dtype) for x in shapes] + [S((4,)), S((4,))],
    )(*out)
    return out[0], out[1].T, out[2][None], out[3][None]


def solution(mesh):
    return jax.shard_map(
        per_device,
        mesh=mesh,
        in_specs=(
            P(("dp", "expert"), None),
            P(("dp", "expert"), None),
            P(("dp", "expert"), None),
            P(("dp", "expert"), None),
            P("expert", None, None),
            P("expert", None, None),
        ),
        out_specs=(
            P(("dp", "expert"), None),
            P(("dp", "expert"), None),
            P("expert", "dp", None),
            P("expert", "dp", None),
        ),
        check_vma=False,
    )
```

```python
import functools

import jax
import jax.numpy as jnp
from jax import lax
from jax.experimental import pallas as pl
from jax.experimental.pallas import tpu as pltpu
from jax.sharding import PartitionSpec as P

F32 = jnp.float32
BF16 = jnp.bfloat16
MESH = pl.DeviceIdType.MESH

NX, NY, NZ = 4, 8, 12
TOK = 40
DM = 2048
FF = 512
AG_ROWS = (416, 400)
RS_ROWS = (336, 320)
CA = 640
CB = 2 * FF - CA
ORDER = (
    ("F5",), ("S5", 1), ("F6",), ("W", 4), ("BY", 0, 4, 1), ("BY", 1, 4, 0), ("S6", 0), ("S6", 1),
    ("W", 3), ("BY", 1, 3, 1), ("W", 5), ("BY", 0, 3, 0), ("S5", 0), ("Z", 1, 6, 1), ("A2", 0, 4),
    ("A2", 1, 4), ("Z", 1, 6, 0), ("Z", 0, 6, 3), ("Z", 1, 5, 2), ("Z", 0, 6, 2), ("W", 2),
    ("BY", 1, 3, 0), ("BY", 0, 3, 1), ("Z", 1, 5, 3), ("A2", 0, 3), ("Z", 0, 5, 0), ("A2", 1, 5),
    ("Z", 0, 5, 1), ("W", 6), ("BY", 1, 2, 1), ("Z", 1, 5, 1), ("BY", 0, 2, 0), ("Z", 0, 5, 3),
    ("A2", 1, 3), ("A2", 0, 5), ("Z", 1, 5, 0), ("A3", 4), ("Z", 0, 5, 2), ("Z", 1, 4, 2),
    ("W", 1), ("Z", 0, 4, 0), ("BY", 1, 2, 0), ("A2", 1, 2), ("Z", 1, 4, 3), ("BY", 0, 2, 1),
    ("Z", 0, 4, 1), ("Z", 1, 4, 1), ("A2", 0, 2), ("Z", 0, 4, 3), ("W", 7), ("Z", 1, 4, 0),
    ("BY", 1, 1, 1), ("BY", 0, 1, 0), ("Z", 0, 4, 2), ("Z", 1, 3, 2), ("Z", 0, 3, 0), ("A3", 3),
    ("AY", 1, 3), ("A2", 0, 6), ("Z", 1, 3, 3), ("A2", 1, 6), ("Z", 0, 3, 1), ("A3", 5),
    ("A2", 1, 1), ("AY", 0, 3), ("Z", 1, 3, 1), ("Z", 0, 3, 3), ("W", 0), ("Z", 1, 3, 0),
    ("BY", 1, 1, 0), ("BY", 0, 1, 1), ("Z", 0, 3, 2), ("A2", 0, 1), ("A2", 1, 7), ("Z", 1, 2, 2),
    ("Z", 0, 2, 0), ("Z", 1, 2, 3), ("A3", 2), ("Z", 0, 2, 1), ("A2", 0, 7), ("A3", 6),
    ("Z", 1, 2, 1), ("AY", 1, 2), ("AY", 0, 2), ("Z", 0, 2, 3), ("Z", 1, 2, 0), ("Z", 0, 2, 2),
    ("Z", 1, 1, 2), ("Z", 0, 1, 0), ("BS",), ("Z", 1, 1, 3), ("A2", 0, 0), ("Z", 0, 1, 1),
    ("A3", 1), ("Z", 1, 1, 1), ("A2", 1, 0), ("A3", 7), ("AY", 1, 1), ("AY", 0, 1),
    ("Z", 0, 1, 3), ("Z", 1, 1, 0), ("Z", 0, 1, 2), ("BX", 1), ("BX", 0), ("ZF", 1), ("ZF", 3),
    ("A3", 0), ("ZF", 0), ("AF",), ("ZF", 2), ("BF",),
)
NT = (((1,), (1,)), ((), ()))
TN = (((0,), (0,)), ((), ()))


def dot(a, b, dims=(((1,), (0,)), ((), ()))):
    return lax.dot_general(a, b, dims, preferred_element_type=F32)


def iota(shape, dim):
    return lax.broadcasted_iota(jnp.int32, shape, dim)


def kernel(
    tok_in, go_in, routes_in, comb_in, wg, wu,
    gt_out, gc_out, dg_out, du_out,
    tok, go, routes, comb, gt, gc, dg, du,
    ZR, ZS, X, GU, WC, OWN, SND, SIB, RP, RM,
    PA, PB, AX1, AX2, SA, SAB, AY1, AY, BY, SB, SBB, BX1, BX2, BXS,
    w_sem, in_sem, out_sem,
    ag_send, zr_recv, sf_send, zs_recv, snd_send, sib_recv, rs_send, rs_recv,
    ax1_send, ax1_recv, ax2_send, ax2_recv, ay_send, ay_recv, by_send, by_recv,
    bx1_send, bx1_recv, bx2_send, bx2_recv,
):
    dp = lax.axis_index("dp")
    ex = lax.axis_index("expert")
    x, y = lax.rem(dp, NX), dp // NX
    core, z = lax.rem(ex, 2), ex // 2

    def xdev(step):
        return (y * NX + lax.rem(x + step + NX, NX), ex)

    def ydev(step):
        return (lax.rem(y + step + NY, NY) * NX + x, ex)

    def zdev(step):
        return (dp, lax.rem(z + step + NZ, NZ) * 2 + core)

    sib = (dp, z * 2 + 1 - core)

    def remote(src, dst, ssem, rsem, dev):
        return pltpu.make_async_remote_copy(
            src_ref=src, dst_ref=dst, send_sem=ssem, recv_sem=rsem,
            device_id=dev, device_id_type=MESH,
        )

    barrier = pltpu.get_barrier_semaphore()
    for dev in (zdev(1), zdev(-1), sib, xdev(1), xdev(-1), ydev(1), ydev(-1)):
        pl.semaphore_signal(barrier, inc=1, device_id=dev, device_id_type=MESH)

    loads = [
        pltpu.make_async_copy(src, dst, in_sem.at[i])
        for i, (src, dst) in enumerate(
            ((tok_in, tok), (go_in, go), (routes_in, routes), (comb_in, comb))
        )
    ]
    stores = [
        pltpu.make_async_copy(src, dst, out_sem.at[i])
        for i, (src, dst) in enumerate(((gt, gt_out), (gc, gc_out), (dg, dg_out), (du, du_out)))
    ]
    load_g = pltpu.make_async_copy(wg.at[0], WC.at[:, pl.ds(0, FF)], w_sem.at[0])
    load_u = pltpu.make_async_copy(wu.at[0], WC.at[:, pl.ds(FF, FF)], w_sem.at[1])
    for load in loads:
        load.start()
    load_g.start()
    load_u.start()
    for load in loads:
        load.wait()

    tf = tok[...].astype(F32)
    gf = go[...].astype(F32)
    for j in range(2):
        for b in range(4):
            lo = j * 512 + b * 128
            ZR[0, j, pl.ds(80 * b, 80), :] = jnp.concatenate(
                [tf[:, lo:lo + 128], tf[:, 1024 + lo:1024 + lo + 128]], axis=0
            ).astype(BF16)
        ZR[0, j, pl.ds(320, 80), :] = jnp.concatenate(
            [gf[:, j * 128:j * 128 + 128], gf[:, 256 + j * 128:256 + j * 128 + 128]], axis=0
        ).astype(BF16)

    def ag(p, k, q):
        j, h = q // 2, q % 2
        rows = pl.ds(208 * h, AG_ROWS[j] - 208 if h else 208)
        if p:
            src, dst = lax.rem(13 - k, NZ), NZ - k
        else:
            src, dst = k - 1, k
        return remote(
            ZR.at[src, j, rows], ZR.at[dst, j, rows],
            ag_send.at[p, k - 1, q], zr_recv.at[dst, q], zdev(1 if p else -1),
        )

    def share(r, j):
        rows = pl.ds(0, AG_ROWS[j])
        return remote(ZR.at[r, j, rows], ZS.at[r, j, rows], sf_send.at[r, j], zs_recv.at[r, j], sib)

    def give(r, j):
        rows = pl.ds(0, RS_ROWS[j])
        return remote(SND.at[r, j, rows], SIB.at[r, j, rows], snd_send.at[r, j], sib_recv.at[r, j], sib)

    def part(q):
        return q // 2, pl.ds(160 * (q % 2), 176 if q == 1 else 160)

    def rs(p, k, q):
        j, rows = part(q)
        src = k if p else NZ - k
        land = RP if p else RM
        return remote(
            OWN.at[src, j, rows], land.at[k - 1, j, rows],
            rs_send.at[p, k - 1, q], rs_recv.at[p, k - 1, q], zdev(1 if p else -1),
        )

    pl.semaphore_wait(barrier, 7)
    ag(1, 1, 0).start()
    ag(0, 1, 2).start()

    rt = routes[...]
    cf = comb[...].astype(F32)
    r16, r40 = iota((16, TOK), 0), iota((TOK, 128), 0)
    lane = iota((TOK, 128), 1)
    r16w = iota((16, 128), 0)
    spots = [(lane == r40 + c * TOK).astype(BF16) for c in range(2)]
    tile = jnp.zeros((16, 128), F32)
    for c in range(2):
        dense = jnp.zeros((16, TOK), F32)
        for k in range(8):
            dense = dense + jnp.where(rt[k:k + 1, :] == 2 * r16 + c, cf[k:k + 1, :], 0.0)
        tile = tile + dot(dense.astype(BF16), spots[c])
    ZR[0, 0, pl.ds(400, 16), :] = tile.astype(BF16)

    pick = lane == core * TOK + r40

    for q in range(1, 4):
        ag(1, 1, q).start()
        ag(0, 1, (q + 2) % 4).start()
    share(0, 0).start()
    share(0, 1).start()
    load_g.wait()
    load_u.wait()

    def rows_of(slots, j, lo):
        top, low = [], []
        for r in slots:
            for buf in (ZR, ZS):
                block = buf[r, j, pl.ds(lo, 80), :].astype(F32)
                top.append(block[:TOK])
                low.append(block[TOK:])
        return jnp.concatenate(top, axis=0), jnp.concatenate(low, axis=0)

    def gather_rows(slots, row0):
        n = 80 * len(slots)
        rows = pl.ds(row0, n)
        for r in slots:
            for j in range(2):
                share(r, j).wait_recv()
        for j in range(2):
            for b in range(4):
                top, low = rows_of(slots, j, 80 * b)
                X[rows, pl.ds(j * 512 + b * 128, 128)] = top.astype(BF16)
                X[rows, pl.ds(1024 + j * 512 + b * 128, 128)] = low.astype(BF16)
        weights = []
        for r in slots:
            for buf in (ZR, ZS):
                tile = buf[r, 0, pl.ds(400, 16), :].astype(F32)
                line = jnp.sum(jnp.where(r16w == z, tile, 0.0), axis=0, keepdims=True)
                weights.append(jnp.sum(jnp.where(pick, line, 0.0), axis=1, keepdims=True))
        return jnp.concatenate(weights, axis=0)

    def units(slots, row0, t, weight):
        rows = pl.ds(row0, 80 * len(slots))
        cot = jnp.concatenate([rows_of(slots, j, 320)[t] for j in range(2)], axis=1)
        xs = X[rows, :]
        gate = dot(xs, WC[:, pl.ds(256 * t, 256)])
        up = dot(xs, WC[:, pl.ds(FF + 256 * t, 256)])
        sig = 1.0 / (1.0 + jnp.exp(-gate))
        act = gate * sig
        ups = weight * cot
        GU[rows, pl.ds(256 * t, 256)] = (
            ups * up * sig * (1.0 + gate * (1.0 - sig))
        ).astype(BF16)
        GU[rows, pl.ds(FF + 256 * t, 256)] = (ups * act).astype(BF16)
        return jnp.sum(act * up * cot, axis=1, keepdims=True)

    def put_sums(slots, total):
        i = 0
        for r in slots:
            for buf in (OWN, SND):
                line = jnp.sum(
                    jnp.where(pick, total[TOK * i:TOK * i + TOK], 0.0), axis=0, keepdims=True
                )
                buf[r, 0, pl.ds(320, 16), :] = jnp.where(r16w == z, line, 0.0).astype(BF16)
                i += 1

    def first(slots, row0, between=None):
        weight = gather_rows(slots, row0)
        total = units(slots, row0, 0, weight)
        if between is not None:
            between()
        put_sums(slots, total + units(slots, row0, 1, weight))

    def second(slots, row0, j):
        grads = GU[pl.ds(row0, 80 * len(slots)), :]
        top = dot(grads, WC[pl.ds(j * 512, 512), :], NT)
        low = dot(grads, WC[pl.ds(1024 + j * 512, 512), :], NT)
        i = 0
        for r in slots:
            for buf in (OWN, SND):
                for b in range(4):
                    buf[r, j, pl.ds(80 * b, 80), :] = jnp.concatenate(
                        [
                            top[TOK * i:TOK * i + TOK, 128 * b:128 * b + 128],
                            low[TOK * i:TOK * i + TOK, 128 * b:128 * b + 128],
                        ],
                        axis=0,
                    ).astype(BF16)
                i += 1
            give(r, j).start()

    def arrive(k, i):
        for p in (1, 0):
            q = i if p else (i + 2) % 4
            ag(p, k, q).wait_recv()
            if i < 2:
                ag(p, k + 1, q).start()
            else:
                @pl.when(k < 5)
                def _():
                    ag(p, k + 1, q).start()
            if i % 2:
                share(NZ - k if p else k, q // 2).start()

    def pair(k):
        return [NZ - k, k], pl.multiple_of(160 * k - 80, 16)

    arrive(1, 0)
    arrive(1, 1)
    first([0], 0, lambda: arrive(1, 2))
    second([0], 0, 0)
    arrive(1, 3)
    second([0], 0, 1)

    def gather_step(k, carry, old=True):
        arrive(k, 0)
        if old:
            second(*pair(k - 2), 1)
        arrive(k, 1)
        first(*pair(k - 1), lambda: arrive(k, 2))
        arrive(k, 3)
        second(*pair(k - 1), 0)
        return carry

    gather_step(2, 0, False)
    lax.fori_loop(3, 6, gather_step, 0)
    for i in range(2):
        for p in (1, 0):
            ag(p, 6, i if p else i + 2).wait_recv()
            if i:
                share(6, 1 - p).start()
        if i == 0:
            second(*pair(4), 1)

    sent, done = [], []

    def go(copy):
        copy.start()
        sent.append((len(done), copy))

    def weight_rows(dy):
        col = pl.multiple_of(lax.rem(y + dy, NY) * 256, 256)
        xs = X[:, pl.ds(col, 256)]
        PA[dy] = dot(xs, GU[:, pl.ds(0, CA)], TN).astype(BF16)
        PB[dy] = dot(xs, GU[:, pl.ds(CA, CB)], TN).astype(BF16)

    def xrow(step):
        return lax.rem(x + step, NX) * 64

    def near(p):
        return 1 if p else NX - 1

    def ax1(p, dy):
        row = pl.multiple_of(xrow(2) + (0 if p else 32), 32)
        return remote(
            PA.at[dy, pl.ds(row, 32)], AX1.at[p, dy], ax1_send.at[p, dy], ax1_recv.at[p, dy],
            xdev(1 if p else -1),
        )

    def ax2(p, dy):
        row = pl.multiple_of(xrow(near(p)), 64)
        return remote(
            PA.at[dy, pl.ds(row, 64)], AX2.at[p, dy], ax2_send.at[p, dy], ax2_recv.at[p, dy],
            xdev(1 if p else -1),
        )

    def a_open(dy):
        weight_rows(dy)
        go(ax1(1, dy))
        go(ax1(0, dy))

    def a_pass(p, dy):
        ax1(p, dy).wait_recv()
        row = pl.multiple_of(xrow(near(p)) + (0 if p else 32), 32)
        PA[dy, pl.ds(row, 32), :] = (
            PA[dy, pl.ds(row, 32), :].astype(F32) + AX1[p, dy].astype(F32)
        ).astype(BF16)
        go(ax2(p, dy))

    def a_sum(dy):
        ax2(1, dy).wait_recv()
        ax2(0, dy).wait_recv()
        row = pl.multiple_of(x * 64, 64)
        SA[dy] = (
            PA[dy, pl.ds(row, 64), :].astype(F32)
            + AX2[1, dy].astype(F32) + AX2[0, dy].astype(F32)
        )
        if dy == 4:
            SAB[4] = SA[4].astype(BF16)
            go(ay1(1))
            go(ay1(0))

    def ay1(p):
        return remote(
            SAB.at[4, pl.ds(0 if p else 32, 32)], AY1.at[p], ay_send.at[p, 3], ay_recv.at[p, 3],
            ydev(1 if p else -1),
        )

    def ay(p, k):
        return remote(
            SAB.at[k if p else NY - k], AY.at[p, k - 1], ay_send.at[p, k - 1],
            ay_recv.at[p, k - 1], ydev(1 if p else -1),
        )

    def ay_pass(p, k):
        dy = k if p else NY - k
        if k == 3:
            ay1(p).wait_recv()
            lo = 0 if p else 32
            SAB[dy, pl.ds(32 - lo, 32), :] = SA[dy, pl.ds(32 - lo, 32), :].astype(BF16)
            SAB[dy, pl.ds(lo, 32), :] = (
                SA[dy, pl.ds(lo, 32), :] + AY1[p].astype(F32)
            ).astype(BF16)
        else:
            ay(p, k + 1).wait_recv()
            SAB[dy] = (SA[dy] + AY[p, k].astype(F32)).astype(BF16)
        go(ay(p, k))

    def a_last():
        ay(1, 1).wait_recv()
        ay(0, 1).wait_recv()
        total = SA[0] + AY[1, 0].astype(F32) + AY[0, 0].astype(F32)
        dg[...] = total[:, :FF]
        du[:, pl.ds(0, CA - FF)] = total[:, FF:]
        stores[2].start()

    def by(p, k, s):
        dy = k if p else NY - k
        return remote(
            PB.at[dy, pl.ds(128 * s, 128)], BY.at[p, k - 1, s], by_send.at[p, k - 1, s],
            by_recv.at[p, k - 1, s], ydev(1 if p else -1),
        )

    def b_pass(p, k, s):
        dy = k if p else NY - k
        rows = pl.ds(128 * s, 128)
        if k < 3 or (k == 3 and s == 1 - p):
            by(p, k + 1, s).wait_recv()
            PB[dy, rows, :] = (PB[dy, rows, :].astype(F32) + BY[p, k, s].astype(F32)).astype(BF16)
        go(by(p, k, s))

    def b_sum():
        for s in (1, 0):
            by(1, 1, s).wait_recv()
            by(0, 1, s).wait_recv()
            rows = pl.ds(128 * s, 128)
            SB[rows, :] = (
                PB[0, rows, :].astype(F32) + BY[1, 0, s].astype(F32) + BY[0, 0, s].astype(F32)
            )
        row = pl.multiple_of(xrow(2), 64)
        SBB[...] = SB[pl.ds(row, 64), :].astype(BF16)
        go(bx1(1))
        go(bx1(0))

    def bx1(p):
        return remote(
            SBB.at[pl.ds(0 if p else 32, 32)], BX1.at[p], bx1_send.at[p], bx1_recv.at[p],
            xdev(1 if p else -1),
        )

    def bx2(p):
        return remote(
            BXS.at[p], BX2.at[p], bx2_send.at[p], bx2_recv.at[p], xdev(1 if p else -1)
        )

    def bx_pass(p):
        row = pl.multiple_of(xrow(near(p)), 64)
        mine = SB[pl.ds(row, 64), :]
        bx1(p).wait_recv()
        lo = 0 if p else 32
        BXS[p, pl.ds(32 - lo, 32), :] = mine[32 - lo:64 - lo].astype(BF16)
        BXS[p, pl.ds(lo, 32), :] = (mine[lo:lo + 32] + BX1[p].astype(F32)).astype(BF16)
        go(bx2(p))

    def b_last():
        bx2(1).wait_recv()
        bx2(0).wait_recv()
        row = pl.multiple_of(x * 64, 64)
        du[:, pl.ds(CA - FF, CB)] = (
            SB[pl.ds(row, 64), :] + BX2[1].astype(F32) + BX2[0].astype(F32)
        )

    given = set()

    def mix(r, q):
        j, rows = part(q)
        if (r, j) not in given:
            given.add((r, j))
            give(r, j).wait_recv()
        return OWN[r, j, rows, :].astype(F32) + SIB[r, j, rows, :].astype(F32)

    def z_pass(p, k, q):
        r = k if p else NZ - k
        j, rows = part(q)
        total = mix(r, q)
        if k < 5 or (k == 5 and j == 1 - p):
            rs(p, k + 1, q).wait_recv()
            land = RP if p else RM
            total = total + land[k, j, rows, :].astype(F32)
        OWN[r, j, rows, :] = total.astype(BF16)
        go(rs(p, k, q))

    def z_last(q):
        j, rows = part(q)
        rs(1, 1, q).wait_recv()
        rs(0, 1, q).wait_recv()
        total = mix(0, q) + RP[0, j, rows, :].astype(F32) + RM[0, j, rows, :].astype(F32)
        for b in range(2):
            lo = j * 512 + (q % 2 * 2 + b) * 128
            gt[:, pl.ds(lo, 128)] = total[80 * b:80 * b + TOK].astype(BF16)
            gt[:, pl.ds(1024 + lo, 128)] = total[80 * b + TOK:80 * b + 80].astype(BF16)
        if q == 1:
            back = total[160:176].astype(BF16)
            for k in range(8):
                gc[k:k + 1, :] = sum(
                    jnp.sum(
                        jnp.where(rt[k:k + 1, :] == 2 * r16 + c, dot(back, spots[c], NT), 0.0),
                        axis=0, keepdims=True,
                    )
                    for c in range(2)
                ).astype(BF16)
            stores[1].start()

    steps = {
        "F5": lambda: first(*pair(5)),
        "S5": lambda j: second(*pair(5), j),
        "F6": lambda: first([6], 880),
        "S6": lambda j: second([6], 880, j),
        "W": a_open, "A2": a_pass, "A3": a_sum, "AY": ay_pass, "AF": a_last,
        "BY": b_pass, "BS": b_sum, "BX": bx_pass, "BF": b_last,
        "Z": z_pass, "ZF": z_last,
    }
    early = [ag(p, k, q) for k in range(1, 7) for p in (1, 0) for q in range(4)
             if k < 6 or q // 2 == 1 - p]
    early += [share(r, j) for r in range(NZ) for j in range(2)]
    early += [give(r, j) for r in (0, 1, 11, 2, 10, 3, 9, 4, 8, 5, 7, 6) for j in range(2)]
    for name, *where in ORDER:
        steps[name](*where)
        done.append(name)
        if len(done) > 25:
            for copy in early[:2]:
                copy.wait_send()
            early = early[2:]
        while sent and sent[0][0] < len(done) - 55:
            sent.pop(0)[1].wait_send()
    stores[0].start()
    stores[3].start()

    for copy in early + [copy for _, copy in sent]:
        copy.wait_send()
    for store in stores:
        store.wait()


def hand_on(a, b, c, d, e, f, g, h, va, vb, vc, vd, sem, sem2):
    gets = [
        pltpu.make_async_copy(src, dst, sem.at[i])
        for i, (src, dst) in enumerate(((a, va), (b, vb), (c, vc), (d, vd)))
    ]
    puts = [
        pltpu.make_async_copy(src, dst, sem2.at[i])
        for i, (src, dst) in enumerate(((va, e), (vb, f), (vc, g), (vd, h)))
    ]
    for get in gets:
        get.start()
    for get, put in zip(gets, puts):
        get.wait()
        put.start()
    for put in puts:
        put.wait()


def per_device(tokens, grad_out, routes, combine, w_gate, w_up):
    hbm = pl.BlockSpec(memory_space=pl.ANY)
    V = pltpu.VMEM
    S = pltpu.SemaphoreType.DMA
    shapes = (
        jax.ShapeDtypeStruct((TOK, DM), BF16),
        jax.ShapeDtypeStruct((8, TOK), BF16),
        jax.ShapeDtypeStruct((64, FF), F32),
        jax.ShapeDtypeStruct((64, FF), F32),
    )
    out = pl.pallas_call(
        kernel,
        out_shape=shapes,
        in_specs=[pl.BlockSpec(memory_space=pltpu.HBM)] * 6,
        out_specs=(hbm,) * 4,
        scratch_shapes=[
            V((TOK, DM), BF16),
            V((TOK, FF), BF16),
            V((8, TOK), jnp.int32),
            V((8, TOK), BF16),
            V((TOK, DM), BF16),
            V((8, TOK), BF16),
            V((64, FF), F32),
            V((64, FF), F32),
            V((NZ, 2, 416, 128), BF16),
            V((NZ, 2, 416, 128), BF16),
            V((NZ * 80, DM), BF16),
            V((NZ * 80, 2 * FF), BF16),
            V((DM, 2 * FF), BF16),
            V((NZ, 2, 336, 128), BF16),
            V((NZ, 2, 336, 128), BF16),
            V((NZ, 2, 336, 128), BF16),
            V((6, 2, 336, 128), BF16),
            V((6, 2, 336, 128), BF16),
            V((NY, 256, CA), BF16),
            V((NY, 256, CB), BF16),
            V((2, NY, 32, CA), BF16),
            V((2, NY, 64, CA), BF16),
            V((NY, 64, CA), F32),
            V((NY, 64, CA), BF16),
            V((2, 32, CA), BF16),
            V((2, 3, 64, CA), BF16),
            V((2, 4, 2, 128, CB), BF16),
            V((256, CB), F32),
            V((64, CB), BF16),
            V((2, 32, CB), BF16),
            V((2, 64, CB), BF16),
            V((2, 64, CB), BF16),
            S((2,)), S((4,)), S((4,)),
            S((2, 6, 4)), S((NZ, 4)), S((NZ, 2)), S((NZ, 2)), S((NZ, 2)), S((NZ, 2)),
            S((2, 6, 4)), S((2, 6, 4)),
            S((2, NY)), S((2, NY)), S((2, NY)), S((2, NY)), S((2, 4)), S((2, 4)),
            S((2, 4, 2)), S((2, 4, 2)),
            S((2,)), S((2,)), S((2,)), S((2,)),
        ],
        compiler_params=pltpu.CompilerParams(
            collective_id=0, has_side_effects=True, vmem_limit_bytes=56 * 2**20
        ),
    )(tokens, grad_out, routes.T, combine.T, w_gate, w_up)
    out = pl.pallas_call(
        hand_on,
        out_shape=shapes,
        in_specs=[hbm] * 4,
        out_specs=(hbm,) * 4,
        scratch_shapes=[V(x.shape, x.dtype) for x in shapes] + [S((4,)), S((4,))],
    )(*out)
    return out[0], out[1].T, out[2][None], out[3][None]


def solution(mesh):
    return jax.shard_map(
        per_device,
        mesh=mesh,
        in_specs=(
            P(("dp", "expert"), None),
            P(("dp", "expert"), None),
            P(("dp", "expert"), None),
            P(("dp", "expert"), None),
            P("expert", None, None),
            P("expert", None, None),
        ),
        out_specs=(
            P(("dp", "expert"), None),
            P(("dp", "expert"), None),
            P("expert", "dp", None),
            P("expert", "dp", None),
        ),
        check_vma=False,
    )
```
